256 devices in a mesh: chain: 8 (over z), op: 32 (over y, x, core).
Axes of the slice: x: 4, y: 4, z: 8, core: 2. Of those that a mesh axis runs over, the one named last changes fastest.
Arguments:
- start_state: float32 [8, 2048, 128], P('chain'), may hold values from -6 to 6
- diagonal: float32 [8, 2048, 128], P('chain'), may hold values from -4 to 4
- left_ops: float32 [8, 128, 16, 128, 128], P('chain', 'op'), may hold values from -0.25 to 0.25
- right_ops: float32 [8, 128, 16, 128, 128], P('chain', 'op'), may hold values from -0.25 to 0.25
- coupling: int32 [8, 128, 16], P('chain', 'op'), may hold values from 0 to 15
- integrals: float32 [128, 32], P('op'), may hold values from -6 to 6
Outputs:
- wavefunction: float32 [8, 2048, 128], P('chain', 'op')
- environment: float32 [8, 32, 128, 128], P('chain', 'op')
The draws below stay inside these ranges and needn't reach their ends.
Inputs may be any that keep to these rules, and one draw needn't show every extreme that they name: `coupling`: each entry names a tile of the same segment's wavefunction.
All inputs are finite; a program needn't handle non-finite values.
Results may differ from the reference program's by a relative error of at most 0.0003.
Values sent between devices are 32-bit elements; how exact they have to be, the bound alone decides.
No kernel may reach another device: no remote copies, remote signals or barrier semaphores. Data moves between devices by JAX's collectives and lax.ppermute only.
A program may use at most 128 MiB of HBM per device.

```python
import jax
import jax.numpy as jnp
from jax import lax

TILE = 128
NBLK = 16
ITERS = 4
CHAINS = 8
TERMS = 128
NEWOPS = 32
ROWS = 2048


def with_ends(drawn, stream_key, least, top_value):
    shape = drawn.shape
    index_at = [jax.random.randint(jax.random.fold_in(stream_key, axis), (), 0, shape[axis]) for axis in range(len(shape))]
    drawn = drawn.at[tuple(index_at)].set(least)
    longest = shape.index(max(shape))
    index_at[longest] = (index_at[longest] + 1) % shape[longest]
    return drawn.at[tuple(index_at)].set(top_value)


def spiked(entries, key, source, target, blocks, factor):
    def block_of(axis_at):
        return (jnp.arange(entries.shape[axis_at]) // (entries.shape[axis_at] // blocks)).reshape((-1,) + (1,) * (entries.ndim - 1 - axis_at))

    near = jax.random.permutation(key, blocks)[block_of(target)]
    far = (block_of(target) + blocks // 2) % blocks
    return jnp.where((block_of(source) == near) | (block_of(source) == far), factor * entries, entries)


def level_of(own_key, dims, split, low, high):
    gain = 1.0
    for axis_at, shards_of in split:
        heights = jax.random.uniform(jax.random.fold_in(jax.random.fold_in(own_key, 6), axis_at), (shards_of,), jnp.float32, low / len(split), high / len(split))
        gain = gain * jnp.repeat(jnp.exp(heights), dims[axis_at] // shards_of).reshape((-1,) + (1,) * (len(dims) - 1 - axis_at))
    return gain


def normal_values(stream_key, extent, width, limit, split=(), kind=jnp.bfloat16):
    array = jax.random.normal(stream_key, extent, jnp.float32) * width
    if len(split) > 0:
        array = level_of(stream_key, extent, split, -0.22, 0.18) * array
    return jnp.clip(array, min=-limit, max=limit).astype(kind)


def gaussian_with(rng, dims, scale, reach, split, heavy, kind=jnp.bfloat16):
    result = scale * jax.random.normal(rng, dims, jnp.float32)
    if split:
        result = result * level_of(rng, dims, split, -0.22, 0.18)
    return jnp.clip(spiked(result, jax.random.fold_in(rng, 3), *heavy), -reach, reach).astype(kind)


def setup_inputs(seed: int = 0) -> dict:
    seeds = jax.random.split(jax.random.key(seed), 7)
    start_state = normal_values(seeds[0], (CHAINS, ROWS, TILE), 1.0, 6.0, ((0, 8),), jnp.float32)
    diagonal = jnp.clip(jax.random.uniform(seeds[1], (CHAINS, ROWS, TILE), jnp.float32, -4.0, 4.0) * level_of(seeds[1], (CHAINS, ROWS, TILE), ((0, 8),), -0.4, 0.0), -4.0, 4.0)
    left_ops = normal_values(seeds[2], (CHAINS, TERMS, NBLK, TILE, TILE), (4 * TILE) ** -0.5, 0.25, ((0, 8), (1, 32)), jnp.float32)
    right_ops = normal_values(seeds[3], (CHAINS, TERMS, NBLK, TILE, TILE), (4 * TILE) ** -0.5, 0.25, ((0, 8), (1, 32)), jnp.float32)
    coupling = with_ends(jax.random.randint(seeds[4], (CHAINS, TERMS, NBLK), 0, NBLK), jax.random.fold_in(seeds[4], 1), 0, NBLK - 1).astype(jnp.int32)
    integrals = gaussian_with(seeds[5], (TERMS, NEWOPS), 1.0, 6.0, ((0, 32),), (0, 1, 32, 2.75), jnp.float32)
    return {"start_state": start_state, "diagonal": diagonal, "left_ops": left_ops, "right_ops": right_ops, "coupling": coupling, "integrals": integrals}


def apply_ham(vector, diag_part, left, right, table):
    blocks = vector.reshape(NBLK, TILE, TILE)

    def add_term(total, item):
        left_tile, right_tile, picks = item
        picked = blocks[picks]
        inner = jnp.einsum('bij,blj->bil', picked, right_tile, precision=lax.Precision.HIGHEST)
        return (total + jnp.einsum('bij,bjl->bil', left_tile, inner, precision=lax.Precision.HIGHEST), None)
    total, unused = lax.scan(add_term, jnp.zeros((NBLK, TILE, TILE), jnp.float32), (left, right, table))
    return total.reshape(ROWS, TILE) + diag_part * vector

def inner_mean(first_arr, second_arr):
    return jnp.mean(first_arr * second_arr)

def segment_solve(start, diag_part, left, right, table):
    state = start / jnp.sqrt(inner_mean(start, start) + 1e-06)
    sigma = apply_ham(state, diag_part, left, right, table)
    theta = inner_mean(state, sigma)
    for step in range(ITERS):
        resid = sigma - theta * state
        precond = resid / jnp.sqrt((diag_part - theta) ** 2 + 1.0)
        proj = inner_mean(state, precond)
        spread = precond - proj * state
        direct = spread / jnp.sqrt(inner_mean(spread, spread) + 1e-06)
        hdirect = apply_ham(direct, diag_part, left, right, table)
        bval = inner_mean(direct, hdirect)
        cval = inner_mean(state, hdirect)
        root = jnp.sqrt(((theta - bval) / 2.0) ** 2 + cval ** 2)
        lam = (theta + bval) / 2.0 - root
        first = bval - lam
        norm = jnp.sqrt(first ** 2 + cval ** 2 + 1e-12)
        state = (first * state - cval * direct) / norm
        sigma = (first * sigma - cval * hdirect) / norm
        theta = lam
    return state

def renormalize(state, left, table, integrals):
    blocks = state.reshape(NBLK, TILE, TILE)

    def one_term(item):
        left_tile, picks = item
        picked = blocks[picks]
        moved = jnp.einsum('bjl,blm->bjm', left_tile, picked, precision=lax.Precision.HIGHEST)
        return jnp.einsum('bji,bjm->im', blocks, moved, precision=lax.Precision.HIGHEST) / TILE
    renorm = lax.map(one_term, (left, table))
    return jnp.einsum('kj,kab->jab', integrals, renorm, precision=lax.Precision.HIGHEST)

def reference(start_state, diagonal, left_ops, right_ops, coupling, integrals):
    waves = []
    newops = []
    for seg in range(CHAINS):
        state = segment_solve(start_state[seg], diagonal[seg], left_ops[seg], right_ops[seg], coupling[seg])
        waves.append(state)
        newops.append(renormalize(state, left_ops[seg], coupling[seg], integrals))
    environment = jnp.cumsum(jnp.stack(newops), axis=0)
    return (jnp.stack(waves), environment)
```

```python
import functools

import jax
import jax.numpy as jnp
from jax import lax
from jax.experimental import pallas as pl
from jax.experimental.pallas import tpu as pltpu
from jax.sharding import PartitionSpec as P

ITERS = 4
T = 128
NB = 16
NK = 4
ROWS = NB * T
HALF = ROWS // 2
PIECE = HALF // 4
COUNT = float(ROWS * T)
BF = jnp.bfloat16
F32 = jnp.float32
VMEM = pl.BlockSpec(memory_space=pltpu.VMEM)
SMEM = pl.BlockSpec(memory_space=pltpu.SMEM)
PARAMS = pltpu.CompilerParams(vmem_limit_bytes=40 << 20)


def shape(*dims, dtype=F32):
    return jax.ShapeDtypeStruct(dims, dtype)


def place(y, x, c):
    return (y * 4 + x) * 2 + c


def line_pairs(m, first):
    pairs = []
    for y in range(4):
        for x in range(4):
            for c in range(2):
                along_x = (c == 0) == first
                to = place(y, x ^ m, c) if along_x else place(y ^ m, x, c)
                pairs.append((place(y, x, c), to))
    return pairs


CORE_PAIRS = [(i, i ^ 1) for i in range(32)]


def split(value):
    high = value.astype(BF)
    low = (value - high.astype(F32)).astype(BF)
    return high, low


def dot(a, b):
    return jnp.dot(a, b, preferred_element_type=F32)


def total(acc):
    return jnp.sum(jnp.sum(acc, axis=0, keepdims=True), axis=1, keepdims=True)


def fold(value):
    return jnp.sum(value.reshape(-1, 8, T), axis=0)


def chunks():
    return [pl.ds(i * PIECE, PIECE) for i in range(ROWS // PIECE)]


def prep_kernel(left, right, lc, rc):
    for k in range(NK):
        high, low = split(left[k, 0])
        lc[0, 0:T, k * T : (k + 1) * T] = high
        lc[0, T : 2 * T, k * T : (k + 1) * T] = low
        high, low = split(right[k, 0].T)
        rc[0, k, :, 0:T] = high
        rc[0, k, :, T : 2 * T] = low


def prep(left, right):
    return pl.pallas_call(
        prep_kernel,
        grid=(NB,),
        in_specs=[pl.BlockSpec((NK, 1, T, T), lambda b: (0, b, 0, 0))] * 2,
        out_specs=[
            pl.BlockSpec((1, 2 * T, NK * T), lambda b: (b, 0, 0)),
            pl.BlockSpec((1, NK, T, 2 * T), lambda b: (b, 0, 0, 0)),
        ],
        out_shape=[shape(NB, 2 * T, NK * T, dtype=BF), shape(NB, NK, T, 2 * T, dtype=BF)],
        compiler_params=PARAMS,
        name="prep",
    )(left, right)


def tile_terms(b, table, vc, lc, rc):
    parts = []
    for k in range(NK):
        picked = vc[table[k, b]]
        weights = jnp.concatenate([rc[b, k], rc[b, k]], axis=0)
        wide = dot(picked, weights)
        parts.append(jnp.concatenate(split(wide[:, :T] + wide[:, T:]), axis=1))
    wide = dot(lc[b], jnp.concatenate(parts, axis=0))
    return wide[:T, :T] + (wide[:T, T:] + wide[T:, :T])


def half_terms(which, table, vc, lc, rc, out):
    for j in range(NB // 2):
        out[j * T : (j + 1) * T, :] = tile_terms(which * (NB // 2) + j, table, vc, lc, rc)


def store_split(vc, chunk, value):
    high, low = split(value)
    for i in range(PIECE // T):
        vc[chunk * (PIECE // T) + i, :, 0:T] = high[i * T : (i + 1) * T]
        vc[chunk * (PIECE // T) + i, :, T : 2 * T] = low[i * T : (i + 1) * T]


def keep_kernel(info, table, vc, lc, rc, out):
    half_terms(info[0], table, vc, lc, rc, out)


def start_kernel(info, table, start, lc, rc, send, vc, state):
    acc = jnp.zeros((8, T), F32)
    for at in chunks():
        value = start[at, :]
        acc += fold(value * value)
    scale = lax.rsqrt(total(acc) / COUNT + 1e-6)
    for i, at in enumerate(chunks()):
        value = start[at, :] * scale
        state[at, :] = value
        store_split(vc, i, value)
    half_terms(1 - info[0], table, vc, lc, rc, send)


def offsets(info):
    own, other = info[0] * HALF, (1 - info[0]) * HALF
    places = [own + (info[1] ^ m) * PIECE for m in range(4)]
    places += [other + (info[2] ^ m) * PIECE for m in range(4)]
    return [pl.ds(pl.multiple_of(at, PIECE), PIECE) for at in places]


def next_direct(state, sigma_at, theta, diag, pre, direct, vc):
    acc = jnp.zeros((8, T), F32)
    for i, at in enumerate(chunks()):
        st, sg = sigma_at(i, at)
        away = diag[at, :] - theta
        value = (sg - theta * st) * lax.rsqrt(away * away + 1.0)
        pre[at, :] = value
        acc += fold(st * value)
    proj = total(acc) / COUNT
    acc = jnp.zeros((8, T), F32)
    for at in chunks():
        value = pre[at, :] - proj * state[at, :]
        pre[at, :] = value
        acc += fold(value * value)
    scale = lax.rsqrt(total(acc) / COUNT + 1e-6)
    for i, at in enumerate(chunks()):
        value = pre[at, :] * scale
        direct[at, :] = value
        store_split(vc, i, value)


def gathered(info, pieces, vector, other, diag, result):
    acc_v, acc_o = jnp.zeros((8, T), F32), jnp.zeros((8, T), F32)
    for piece, at in zip(pieces, offsets(info), strict=True):
        vec = vector[at, :]
        value = piece[...] + diag[at, :] * vec
        result[at, :] = value
        acc_v += fold(vec * value)
        if other is not None:
            acc_o += fold(other[at, :] * value)
    return total(acc_v) / COUNT, total(acc_o) / COUNT


def rotation(theta, bval, cval):
    gap = (theta - bval) / 2.0
    root = jnp.sqrt(gap * gap + cval * cval)
    lam = (theta + bval) / 2.0 - root
    first = bval - lam
    inverse = lax.rsqrt(first * first + cval * cval + 1e-12)
    return lam, first * inverse, cval * inverse


def partial_products(state, direct, diag, table, vc, lc, rc, scal):
    acc_b, acc_c = jnp.zeros((8, T), F32), jnp.zeros((8, T), F32)
    for at in chunks():
        vec = direct[at, :]
        value = (1.0 / 32) * (diag[at, :] * vec)
        acc_b += fold(vec * value)
        acc_c += fold(state[at, :] * value)
    for b in range(NB):
        at = pl.ds(b * T, T)
        value = tile_terms(b, table, vc, lc, rc)
        acc_b += fold(direct[at, :] * value)
        acc_c += fold(state[at, :] * value)
    scal[...] = jnp.zeros_like(scal)
    scal[0:1, :] = jnp.sum(acc_b, axis=0, keepdims=True)
    scal[1:2, :] = jnp.sum(acc_c, axis=0, keepdims=True)


def first_kernel(info, table, *refs):
    pieces, (state, diag, lc, rc, send, vc, sigma, direct, theta_out, pre) = refs[:8], refs[8:]
    theta, _ = gathered(info, pieces, state, None, diag, sigma)
    theta_out[...] = jnp.broadcast_to(theta, theta_out.shape)
    next_direct(state, lambda i, at: (state[at, :], sigma[at, :]), theta, diag, pre, direct, vc)
    half_terms(1 - info[0], table, vc, lc, rc, send)


def step_kernel(last, info, table, *refs):
    pieces, refs = refs[:8], refs[8:]
    state, sigma, direct, theta, diag, lc, rc = refs[:7]
    out, vc, state_out, sigma_out, direct_out, theta_out, pre, hdirect = refs[7:]
    bval, cval = gathered(info, pieces, direct, state, diag, hdirect)
    lam, first, second = rotation(theta[0:1, 0:1], bval, cval)
    theta_out[...] = jnp.broadcast_to(lam, theta_out.shape)

    def updated(i, at):
        st = first * state[at, :] - second * direct[at, :]
        sg = first * sigma[at, :] - second * hdirect[at, :]
        state_out[at, :] = st
        sigma_out[at, :] = sg
        return st, sg

    next_direct(state_out, updated, lam, diag, pre, direct_out, vc)
    if last:
        partial_products(state_out, direct_out, diag, table, vc, lc, rc, out)
    else:
        half_terms(1 - info[0], table, vc, lc, rc, out)


VECTOR = shape(ROWS, T)
SPLIT = shape(NB, T, 2 * T, dtype=BF)
SCALAR = shape(8, T)


def call(kernel, name, n_smem, args, outs, scratch=(), flops=0):
    return pl.pallas_call(
        kernel,
        in_specs=[SMEM] * n_smem + [VMEM] * (len(args) - n_smem),
        out_specs=[VMEM] * len(outs),
        out_shape=list(outs),
        scratch_shapes=list(scratch),
        compiler_params=PARAMS,
        cost_estimate=pl.CostEstimate(flops=flops, bytes_accessed=1 << 20, transcendentals=0),
        name=name,
    )(*args)


def pieces_kernel(info, keep, got, *outs):
    for m, out in enumerate(outs):
        at = pl.ds(pl.multiple_of((info[1] ^ m) * PIECE, PIECE), PIECE)
        out[...] = keep[at, :] + got[at, :]


def sum4(own, got):
    return (own + got[0]) + (got[1] + got[2])


def sum_terms(info, send, keep):
    got = lax.ppermute(send, "op", CORE_PAIRS)
    mine = call(pieces_kernel, "pieces", 1, (info, keep, got), [shape(PIECE, T)] * 4)
    part = sum4(mine[0], [lax.ppermute(mine[m], "op", line_pairs(m, True)) for m in (1, 2, 3)])
    whole = sum4(part, [lax.ppermute(part, "op", line_pairs(m, False)) for m in (1, 2, 3)])
    own = [whole] + [lax.ppermute(whole, "op", line_pairs(m, True)) for m in (1, 2, 3)]
    return own + [lax.ppermute(piece, "op", CORE_PAIRS) for piece in own]


def renorm_kernel(info, table, scal, state, direct, theta, lc, rows, renorm, final, fc, ft, moved):
    acc = jnp.sum(scal[...], axis=0)
    bval = jnp.sum(acc[0:1, :], axis=1, keepdims=True) / COUNT
    cval = jnp.sum(acc[1:2, :], axis=1, keepdims=True) / COUNT
    _, first, second = rotation(theta[0:1, 0:1], bval, cval)
    for b in range(NB):
        at = pl.ds(b * T, T)
        value = first * state[at, :] - second * direct[at, :]
        final[at, :] = value
        high, low = split(value)
        fc[b, :, 0:T] = high
        fc[b, :, T : 2 * T] = low
        high, low = split(value.T)
        ft[0:T, b * T : (b + 1) * T] = high
        ft[T : 2 * T, b * T : (b + 1) * T] = low
    rows[...] = final[pl.ds(pl.multiple_of(info[3], ROWS // 32), ROWS // 32), :]
    for b in range(NB):
        for k in range(NK):
            wide = dot(lc[b, :, k * T : (k + 1) * T], fc[table[k, b]])
            high, low = split(wide[:T, :T] + (wide[:T, T:] + wide[T:, :T]))
            moved[b * T : (b + 1) * T, 2 * k * T : (2 * k + 1) * T] = high
            moved[b * T : (b + 1) * T, (2 * k + 1) * T : (2 * k + 2) * T] = low
    for k in range(NK):
        wide = dot(ft[...], moved[:, 2 * k * T : (2 * k + 2) * T])
        renorm[k] = (wide[:T, :T] + (wide[:T, T:] + wide[T:, :T])) * (1.0 / T)


def newop_kernel(info, own_weights, other_weights, own, other, out):
    for p in range(16):
        acc = None
        for k in range(NK):
            for weights, renorm in ((own_weights, own), (other_weights, other)):
                term = weights[k, 2 * p + info[0]] * renorm[k]
                acc = term if acc is None else acc + term
        out[p] = acc


def per_device(start_state, diagonal, left_ops, right_ops, coupling, integrals):
    start, diag, table = start_state[0], diagonal[0], coupling[0]
    op = lax.axis_index("op")
    core, x, y = op % 2, (op // 2) % 4, op // 8
    info = jnp.stack(
        [core, jnp.where(core == 0, x, y), jnp.where(core == 0, y, x), op * (ROWS // 32)]
    ).astype(jnp.int32)
    other_integrals = lax.ppermute(integrals, "op", CORE_PAIRS)
    lc, rc = prep(left_ops[0], right_ops[0])

    def keep_half(vc):
        return call(
            keep_kernel, "keep", 2, (info, table, vc, lc, rc), [shape(HALF, T)], flops=1 << 31
        )[0]

    send, vc, state = call(
        start_kernel,
        "start",
        2,
        (info, table, start, lc, rc),
        [shape(HALF, T), SPLIT, VECTOR],
    )
    pieces = sum_terms(info, send, keep_half(vc))
    send, vc, sigma, direct, theta = call(
        first_kernel,
        "first",
        2,
        (info, table, *pieces, state, diag, lc, rc),
        [shape(HALF, T), SPLIT, VECTOR, VECTOR, SCALAR],
        [pltpu.VMEM((ROWS, T), F32)],
    )
    for step in range(1, ITERS):
        pieces = sum_terms(info, send, keep_half(vc))
        last = step == ITERS - 1
        send, vc, state, sigma, direct, theta = call(
            functools.partial(step_kernel, last),
            "last" if last else "step",
            2,
            (info, table, *pieces, state, sigma, direct, theta, diag, lc, rc),
            [SCALAR if last else shape(HALF, T), SPLIT, VECTOR, VECTOR, VECTOR, SCALAR],
            [pltpu.VMEM((ROWS, T), F32)] * 2,
        )
    scal = lax.all_to_all(jnp.broadcast_to(send[None], (32, 8, T)), "op", 0, 0)
    own_rows, renorm = call(
        renorm_kernel,
        "renorm",
        2,
        (info, table, scal, state, direct, theta, lc),
        [shape(ROWS // 32, T), shape(NK, T, T)],
        [
            pltpu.VMEM((ROWS, T), F32),
            pltpu.VMEM((NB, T, 2 * T), BF),
            pltpu.VMEM((2 * T, ROWS), BF),
            pltpu.VMEM((ROWS, 2 * NK * T), BF),
        ],
    )
    other = lax.ppermute(renorm, "op", CORE_PAIRS)
    newops = call(
        newop_kernel,
        "newops",
        3,
        (info, integrals, other_integrals, renorm, other),
        [shape(16, T, T)],
    )[0]
    groups = [[2 * p + c for p in range(16)] for c in range(2)]
    shares = lax.all_to_all(newops, "op", 0, 0, axis_index_groups=groups)
    newop = jnp.sum(shares, axis=0)
    within = lax.axis_index("chain") % 4
    got = [
        lax.ppermute(newop, "chain", [(i, i ^ m) for i in range(8)]) for m in (1, 2, 3)
    ]
    lower = lax.ppermute(sum4(newop, got), "chain", [(i, 7 - i) for i in range(4)])
    environment = newop + lower
    for m in (1, 2, 3):
        environment += jnp.where((within ^ m) < within, got[m - 1], 0.0)
    return (own_rows[None], environment[None, None])


def solution(mesh):
    placed = (
        P("chain", None, None),
        P("chain", None, None),
        P("chain", "op", None, None, None),
        P("chain", "op", None, None, None),
        P("chain", "op", None),
        P("op", None),
    )
    return jax.shard_map(
        per_device,
        mesh=mesh,
        in_specs=placed,
        out_specs=(P("chain", "op", None), P("chain", "op", None, None)),
        check_vma=False,
    )
```

```python
import functools

import jax
import jax.numpy as jnp
from jax import lax
from jax.experimental import pallas as pl
from jax.experimental.pallas import tpu as pltpu
from jax.sharding import PartitionSpec as P

ITERS = 4
T = 128
NB = 16
NK = 4
ROWS = NB * T
HALF = ROWS // 2
HT = NB // 2
PIECE = HALF // 4
COUNT = float(ROWS * T)
BF = jnp.bfloat16
F32 = jnp.float32
VMEM = pl.BlockSpec(memory_space=pltpu.VMEM)
HBM = pl.BlockSpec(memory_space=pltpu.HBM)
SMEM = pl.BlockSpec(memory_space=pltpu.SMEM)


def shape(*dims, dtype=F32):
    return jax.ShapeDtypeStruct(dims, dtype)


def place(y, x, c):
    return (y * 4 + x) * 2 + c


def line_pairs(m, first):
    pairs = []
    for y in range(4):
        for x in range(4):
            for c in range(2):
                along_x = (c == 0) == first
                to = place(y, x ^ m, c) if along_x else place(y ^ m, x, c)
                pairs.append((place(y, x, c), to))
    return pairs


CORE_PAIRS = [(i, i ^ 1) for i in range(32)]


def split(value):
    high = value.astype(BF)
    low = (value - high.astype(F32)).astype(BF)
    return high, low


def dot(a, b):
    return jnp.dot(a, b, preferred_element_type=F32)


def total(acc):
    return jnp.sum(jnp.sum(acc, axis=0, keepdims=True), axis=1, keepdims=True)


def fold(value):
    return jnp.sum(value.reshape(-1, 8, T), axis=0)


STEP = 64


def chunks(rows=ROWS):
    return [pl.ds(i, STEP) for i in range(0, rows, STEP)]


def prepare(left, right, j, lc, rc):
    for k in range(NK):
        high, low = split(left[k, j])
        lc[j, 0:T, k * T : (k + 1) * T] = high
        lc[j, T : 2 * T, k * T : (k + 1) * T] = low
        high, low = split(right[k, j].T)
        rc[j, k, :, 0:T] = high
        rc[j, k, :, T : 2 * T] = low


def tile_terms(b, j, table, vc, lc, rc):
    parts = []
    for k in range(NK):
        picked = vc[table[k, b]]
        weights = jnp.concatenate([rc[j, k], rc[j, k]], axis=0)
        wide = dot(picked, weights)
        parts.append(jnp.concatenate(split(wide[:, :T] + wide[:, T:]), axis=1))
    wide = dot(lc[j], jnp.concatenate(parts, axis=0))
    return wide[:T, :T] + (wide[:T, T:] + wide[T:, :T])


def half_terms(which, table, vc, lc, rc, out):
    for j in range(HT):
        out[j * T : (j + 1) * T, :] = tile_terms(which * HT + j, j, table, vc, lc, rc)


def store_split(vc, row, value):
    high, low = split(value)
    at = pl.ds(row % T, STEP)
    vc[row // T, at, 0:T] = high
    vc[row // T, at, T : 2 * T] = low


def keep_kernel(info, table, vc, lc, rc, out):
    half_terms(info[0], table, vc, lc, rc, out)


def first_keep_kernel(info, table, vc, left, right, out, lc, rc):
    for j in range(HT):
        prepare(left, right, j, lc, rc)
        out[j * T : (j + 1) * T, :] = tile_terms(info[0] * HT + j, j, table, vc, lc, rc)


def start_kernel(info, table, start, left, right, send, vc, state, lc, rc, lkeep, rkeep, lbuf, rbuf, sem, keep_sem):
    own, other = info[0] * HT, (1 - info[0]) * HT
    copies = []
    for j in range(HT):
        pair = (
            pltpu.make_async_copy(right.at[:, other + j], rbuf.at[:, j], sem.at[0, j]),
            pltpu.make_async_copy(left.at[:, other + j], lbuf.at[:, j], sem.at[1, j]),
        )
        for copy in pair:
            copy.start()
        copies.append(pair)
    keeps = []
    for k in range(NK):
        keeps.append(pltpu.make_async_copy(right.at[k, pl.ds(own, HT)], rkeep.at[k], keep_sem.at[0, k]))
        keeps.append(pltpu.make_async_copy(left.at[k, pl.ds(own, HT)], lkeep.at[k], keep_sem.at[1, k]))
    for copy in keeps:
        copy.start()
    acc = jnp.zeros((8, T), F32)
    for at in chunks():
        value = start[at, :]
        acc += fold(value * value)
    scale = lax.rsqrt(total(acc) / COUNT + 1e-6)
    for at in chunks():
        value = start[at, :] * scale
        state[at, :] = value
        store_split(vc, at.start, value)
    for j in range(HT):
        for copy in copies[j]:
            copy.wait()
        prepare(lbuf, rbuf, j, lc, rc)
        send[j * T : (j + 1) * T, :] = tile_terms(other + j, j, table, vc, lc, rc)
    for copy in keeps:
        copy.wait()


def offsets(info):
    own, other = info[0] * HALF, (1 - info[0]) * HALF
    places = [own + (info[1] ^ m) * PIECE for m in range(4)]
    places += [other + (info[2] ^ m) * PIECE for m in range(4)]
    return places


def next_direct(state, sigma_at, theta, diag, pre, direct, vc):
    acc = jnp.zeros((8, T), F32)
    for at in chunks():
        st, sg = sigma_at(at)
        away = diag[at, :] - theta
        value = (sg - theta * st) * lax.rsqrt(away * away + 1.0)
        pre[at, :] = value
        acc += fold(st * value)
    proj = total(acc) / COUNT
    acc = jnp.zeros((8, T), F32)
    for at in chunks():
        value = pre[at, :] - proj * state[at, :]
        pre[at, :] = value
        acc += fold(value * value)
    scale = lax.rsqrt(total(acc) / COUNT + 1e-6)
    for at in chunks():
        value = pre[at, :] * scale
        direct[at, :] = value
        store_split(vc, at.start, value)


def gathered(info, pieces, vector, other, diag, result):
    acc_v, acc_o = jnp.zeros((8, T), F32), jnp.zeros((8, T), F32)
    for piece, begin in zip(pieces, offsets(info), strict=True):
        for here in chunks(PIECE):
            at = pl.ds(pl.multiple_of(begin + here.start, STEP), STEP)
            vec = vector[at, :]
            value = piece[here, :] + diag[at, :] * vec
            result[at, :] = value
            acc_v += fold(vec * value)
            if other is not None:
                acc_o += fold(other[at, :] * value)
    return total(acc_v) / COUNT, total(acc_o) / COUNT


def rotation(theta, bval, cval):
    gap = (theta - bval) / 2.0
    root = jnp.sqrt(gap * gap + cval * cval)
    lam = (theta + bval) / 2.0 - root
    first = bval - lam
    inverse = lax.rsqrt(first * first + cval * cval + 1e-12)
    return lam, first * inverse, cval * inverse


def partial_products(state, direct, diag, table, vc, halves, terms, scal):
    for which, lc, rc in halves:
        for j in range(HT):
            b = which * HT + j
            at = pl.ds(pl.multiple_of(b * T, T), T)
            terms[at, :] = tile_terms(b, j, table, vc, lc, rc)
    acc_b, acc_c = jnp.zeros((8, T), F32), jnp.zeros((8, T), F32)
    for at in chunks():
        vec = direct[at, :]
        value = terms[at, :] + (1.0 / 32) * (diag[at, :] * vec)
        acc_b += fold(vec * value)
        acc_c += fold(state[at, :] * value)
    scal[...] = jnp.zeros_like(scal)
    scal[0:1, :] = jnp.sum(acc_b, axis=0, keepdims=True)
    scal[1:2, :] = jnp.sum(acc_c, axis=0, keepdims=True)


def first_kernel(info, table, *refs):
    pieces, (state, diag, lc, rc, send, vc, sigma, direct, theta_out, pre) = refs[:8], refs[8:]
    theta, _ = gathered(info, pieces, state, None, diag, sigma)
    theta_out[...] = jnp.broadcast_to(theta, theta_out.shape)
    next_direct(state, lambda at: (state[at, :], sigma[at, :]), theta, diag, pre, direct, vc)
    half_terms(1 - info[0], table, vc, lc, rc, send)


def step_kernel(last, info, table, *refs):
    pieces, refs = refs[:8], refs[8:]
    state, sigma, direct, theta, diag, lc, rc = refs[:7]
    refs = refs[7:]
    if last:
        (lkeep, rkeep), refs = refs[:2], refs[2:]
    out, vc, state_out, sigma_out, direct_out, theta_out, pre, hdirect = refs
    bval, cval = gathered(info, pieces, direct, state, diag, hdirect)
    lam, first, second = rotation(theta[0:1, 0:1], bval, cval)
    theta_out[...] = jnp.broadcast_to(lam, theta_out.shape)

    def updated(at):
        st = first * state[at, :] - second * direct[at, :]
        sg = first * sigma[at, :] - second * hdirect[at, :]
        state_out[at, :] = st
        sigma_out[at, :] = sg
        return st, sg

    next_direct(state_out, updated, lam, diag, pre, direct_out, vc)
    if last:
        halves = ((1 - info[0], lc, rc), (info[0], lkeep, rkeep))
        partial_products(state_out, direct_out, diag, table, vc, halves, pre, out)
    else:
        half_terms(1 - info[0], table, vc, lc, rc, out)


VECTOR = shape(ROWS, T)
SPLIT = shape(NB, T, 2 * T, dtype=BF)
SCALAR = shape(8, T)


def call(kernel, name, n_smem, args, outs, scratch=(), flops=0, n_hbm=0, mib=24):
    n_vmem = len(args) - n_smem - n_hbm
    hbm = [pltpu.with_memory_space_constraint(arg, pltpu.HBM) for arg in args[n_smem + n_vmem :]]
    return pl.pallas_call(
        kernel,
        in_specs=[SMEM] * n_smem + [VMEM] * n_vmem + [HBM] * n_hbm,
        out_specs=[VMEM] * len(outs),
        out_shape=[pltpu.VMEM(out.shape, out.dtype) for out in outs],
        scratch_shapes=list(scratch),
        compiler_params=pltpu.CompilerParams(vmem_limit_bytes=mib << 20),
        cost_estimate=pl.CostEstimate(flops=flops, bytes_accessed=1 << 20, transcendentals=0),
        name=name,
    )(*args[: n_smem + n_vmem], *hbm)


def sum4(own, got):
    return (own + got[0]) + (got[2] + got[1])


def along(values, first):
    return [lax.ppermute(values[m], "op", line_pairs(m, first)) for m in (1, 3, 2)]


def cut(value, at, count):
    begin = [at] + [jnp.zeros_like(at)] * (value.ndim - 1)
    return lax.dynamic_slice(value, begin, (count, *value.shape[1:]), allow_negative_indices=False)


def sum_terms(begins, send, keep):
    got = lax.ppermute(send, "op", CORE_PAIRS)

    mine = [cut(keep, at, PIECE) + cut(got, at, PIECE) for at in begins]
    part = sum4(mine[0], along(mine, True))
    whole = sum4(part, along([part] * 4, False))
    got = along([whole] * 4, True)
    own = [whole, got[0], got[2], got[1]]
    return own + [lax.ppermute(value, "op", CORE_PAIRS) for value in own]


def renorm_kernel(info, table, scal, state, direct, theta, lc, lkeep, rows, renorm, final, fc, ft, moved):
    acc = jnp.sum(scal[...], axis=0)
    bval = jnp.sum(acc[0:1, :], axis=1, keepdims=True) / COUNT
    cval = jnp.sum(acc[1:2, :], axis=1, keepdims=True) / COUNT
    _, first, second = rotation(theta[0:1, 0:1], bval, cval)
    for at in chunks():
        value = first * state[at, :] - second * direct[at, :]
        final[at, :] = value
        store_split(fc, at.start, value)
    rows[...] = final[pl.ds(pl.multiple_of(info[3], ROWS // 32), ROWS // 32), :]
    order = [((1 - info[0]) * HT + j, lc, j) for j in range(HT)] + [(info[0] * HT + j, lkeep, j) for j in range(HT)]
    for i, (b, ops, j) in enumerate(order):
        high, low = split(final[pl.ds(pl.multiple_of(b * T, T), T), :].T)
        ft[0:T, i * T : (i + 1) * T] = high
        ft[T : 2 * T, i * T : (i + 1) * T] = low
        for k in range(NK):
            wide = dot(ops[j, :, k * T : (k + 1) * T], fc[table[k, b]])
            high, low = split(wide[:T, :T] + (wide[:T, T:] + wide[T:, :T]))
            moved[i * T : (i + 1) * T, 2 * k * T : (2 * k + 1) * T] = high
            moved[i * T : (i + 1) * T, (2 * k + 1) * T : (2 * k + 2) * T] = low
    for k in range(NK):
        wide = dot(ft[...], moved[:, 2 * k * T : (2 * k + 2) * T])
        renorm[k] = (wide[:T, :T] + (wide[:T, T:] + wide[T:, :T])) * (1.0 / T)


def newop_kernel(info, own_weights, other_weights, own, other, *outs):
    along_t = jnp.where(info[0] == 0, 4, 1)
    along_q = 5 - along_t
    for m, out in enumerate(outs):
        for t in range(4):
            j = 2 * (t * along_t + (info[1] ^ m) * along_q) + info[0]
            acc = None
            for k in range(NK):
                for weights, renorm in ((own_weights, own), (other_weights, other)):
                    term = weights[k, j] * renorm[k]
                    acc = term if acc is None else acc + term
            out[t] = acc


def per_device(start_state, diagonal, left_ops, right_ops, coupling, integrals):
    start, diag, table = start_state[0], diagonal[0], coupling[0]
    op = lax.axis_index("op")
    core, x, y = op % 2, (op // 2) % 4, op // 8
    quarter, other_quarter = jnp.where(core == 0, x, y), jnp.where(core == 0, y, x)
    chain = lax.axis_index("chain")
    info = jnp.stack([core, quarter, other_quarter, op * (ROWS // 32)]).astype(jnp.int32)
    begins = [(quarter ^ m) * PIECE for m in range(4)]
    positions = [other_quarter ^ m for m in range(4)]
    info, begins, positions, odd, upper = lax.optimization_barrier(
        (info, begins, positions, chain % 2 > 0, chain % 4 > 1)
    )
    other_integrals = lax.ppermute(integrals, "op", CORE_PAIRS)
    lc_shape = shape(HT, 2 * T, NK * T, dtype=BF)
    rc_shape = shape(HT, NK, T, 2 * T, dtype=BF)
    raw = (NK, HT, T, T)
    send, vc, state, lc, rc, lraw, rraw = call(
        start_kernel,
        "start",
        2,
        (info, table, start, left_ops[0], right_ops[0]),
        [shape(HALF, T), SPLIT, VECTOR, lc_shape, rc_shape, shape(*raw), shape(*raw)],
        [pltpu.VMEM(raw, F32)] * 2 + [pltpu.SemaphoreType.DMA((2, HT)), pltpu.SemaphoreType.DMA((2, NK))],
        n_hbm=2,
    )
    keep, lkeep, rkeep = call(
        first_keep_kernel,
        "first_keep",
        2,
        (info, table, vc, lraw, rraw),
        [shape(HALF, T), lc_shape, rc_shape],
        flops=1 << 31,
    )
    pieces = sum_terms(begins, send, keep)
    send, vc, sigma, direct, theta = call(
        first_kernel,
        "first",
        2,
        (info, table, *pieces, state, diag, lc, rc),
        [shape(HALF, T), SPLIT, VECTOR, VECTOR, SCALAR],
        [pltpu.VMEM((ROWS, T), F32)],
    )
    for step in range(1, ITERS):
        keep = call(
            keep_kernel, "keep", 2, (info, table, vc, lkeep, rkeep), [shape(HALF, T)], flops=1 << 31
        )[0]
        pieces = sum_terms(begins, send, keep)
        last = step == ITERS - 1
        ops = (lc, rc, lkeep, rkeep) if last else (lc, rc)
        send, vc, state, sigma, direct, theta = call(
            functools.partial(step_kernel, last),
            "last" if last else "step",
            2,
            (info, table, *pieces, state, sigma, direct, theta, diag, *ops),
            [SCALAR if last else shape(HALF, T), SPLIT, VECTOR, VECTOR, VECTOR, SCALAR],
            [pltpu.VMEM((ROWS, T), F32)] * 2,
        )
    groups = [[2 * p + c for p in range(16)] for c in range(2)]
    scal = send + lax.ppermute(send, "op", CORE_PAIRS)
    scal = lax.all_to_all(jnp.broadcast_to(scal[None], (16, 8, T)), "op", 0, 0, axis_index_groups=groups)
    own_rows, renorm = call(
        renorm_kernel,
        "renorm",
        2,
        (info, table, scal, state, direct, theta, lc, lkeep),
        [shape(ROWS // 32, T), shape(NK, T, T)],
        [
            pltpu.VMEM((ROWS, T), F32),
            pltpu.VMEM((NB, T, 2 * T), BF),
            pltpu.VMEM((2 * T, ROWS), BF),
            pltpu.VMEM((ROWS, 2 * NK * T), BF),
        ],
    )
    other = lax.ppermute(renorm, "op", CORE_PAIRS)
    newops = call(
        newop_kernel,
        "newops",
        3,
        (info, integrals, other_integrals, renorm, other),
        [shape(4, T, T)] * 4,
    )
    got = [newops[0]] + along(newops, True)

    def position(at):
        mine, *others = [cut(value, at, 1)[0] for value in got]
        return sum4(mine, others)

    mine = [position(at) for at in positions]
    newop = sum4(mine[0], along(mine, False))
    got = lax.ppermute(newop, "chain", [(i, i ^ 1) for i in range(8)])
    before, pair = jnp.where(odd, got, 0.0), newop + got
    got = lax.ppermute(pair, "chain", [(i, i ^ 2) for i in range(8)])
    before, four = before + jnp.where(upper, got, 0.0), pair + got
    got = lax.ppermute(four, "chain", [(0, 6), (1, 7), (2, 4), (3, 5)])
    environment = newop + before + got
    return (own_rows[None], environment[None, None])


def solution(mesh):
    placed = (
        P("chain", None, None),
        P("chain", None, None),
        P("chain", "op", None, None, None),
        P("chain", "op", None, None, None),
        P("chain", "op", None),
        P("op", None),
    )
    return jax.shard_map(
        per_device,
        mesh=mesh,
        in_specs=placed,
        out_specs=(P("chain", "op", None), P("chain", "op", None, None)),
        check_vma=False,
    )
```

```python
import functools

import jax
import jax.numpy as jnp
from jax import lax
from jax.experimental import pallas as pl
from jax.experimental.pallas import tpu as pltpu
from jax.sharding import PartitionSpec as P

ITERS = 4
T = 128
NB = 16
NK = 4
ROWS = NB * T
HALF = ROWS // 2
HT = NB // 2
PIECE = HALF // 4
COUNT = float(ROWS * T)
BF = jnp.bfloat16
F32 = jnp.float32
VMEM = pl.BlockSpec(memory_space=pltpu.VMEM)
HBM = pl.BlockSpec(memory_space=pltpu.HBM)
SMEM = pl.BlockSpec(memory_space=pltpu.SMEM)


def shape(*dims, dtype=F32):
    return jax.ShapeDtypeStruct(dims, dtype)


def place(y, x, c):
    return (y * 4 + x) * 2 + c


def line_pairs(m, first):
    pairs = []
    for y in range(4):
        for x in range(4):
            for c in range(2):
                along_x = (c == 0) == first
                to = place(y, x ^ m, c) if along_x else place(y ^ m, x, c)
                pairs.append((place(y, x, c), to))
    return pairs


CORE_PAIRS = [(i, i ^ 1) for i in range(32)]


def split(value):
    high = value.astype(BF)
    low = (value - high.astype(F32)).astype(BF)
    return high, low


def dot(a, b):
    return jnp.dot(a, b, preferred_element_type=F32)


def total(acc):
    return jnp.sum(jnp.sum(acc, axis=0, keepdims=True), axis=1, keepdims=True)


def fold(value):
    return jnp.sum(value.reshape(-1, 8, T), axis=0)


STEP = 64


def chunks(rows=ROWS):
    return [pl.ds(i, STEP) for i in range(0, rows, STEP)]


def prepare(left, right, j, lc, rc):
    for k in range(NK):
        high, low = split(left[k, j])
        lc[j, 0:T, k * T : (k + 1) * T] = high
        lc[j, T : 2 * T, k * T : (k + 1) * T] = low
        high, low = split(right[k, j].T)
        rc[j, k, :, 0:T] = high
        rc[j, k, :, T : 2 * T] = low


def tile_terms(b, j, table, vc, lc, rc):
    parts = []
    for k in range(NK):
        picked = vc[table[k, b]]
        weights = jnp.concatenate([rc[j, k], rc[j, k]], axis=0)
        wide = dot(picked, weights)
        parts.append(jnp.concatenate(split(wide[:, :T] + wide[:, T:]), axis=1))
    wide = dot(lc[j], jnp.concatenate(parts, axis=0))
    return wide[:T, :T] + (wide[:T, T:] + wide[T:, :T])


def half_terms(which, table, vc, lc, rc, out):
    for j in range(HT):
        out[j * T : (j + 1) * T, :] = tile_terms(which * HT + j, j, table, vc, lc, rc)


def store_split(vc, row, value):
    high, low = split(value)
    at = pl.ds(row % T, STEP)
    vc[row // T, at, 0:T] = high
    vc[row // T, at, T : 2 * T] = low


def keep_kernel(info, table, vc, lc, rc, out):
    half_terms(info[0], table, vc, lc, rc, out)


def first_keep_kernel(info, table, vc, left, right, out, lc, rc):
    for j in range(HT):
        prepare(left, right, j, lc, rc)
        out[j * T : (j + 1) * T, :] = tile_terms(info[0] * HT + j, j, table, vc, lc, rc)


def start_kernel(
    info, table, start_hbm, left, right, send, vc, state, lc, rc, lkeep, rkeep, start, lbuf, rbuf, start_sem, sem, keep_sem
):
    own, other = info[0] * HT, (1 - info[0]) * HT
    start_copy = pltpu.make_async_copy(start_hbm, start, start_sem)
    sends = [
        (
            pltpu.make_async_copy(right.at[:, other + j], rbuf.at[:, j], sem.at[0, j]),
            pltpu.make_async_copy(left.at[:, other + j], lbuf.at[:, j], sem.at[1, j]),
        )
        for j in range(HT)
    ]
    keeps = [
        (
            pltpu.make_async_copy(right.at[:, own + j], rkeep.at[:, j], keep_sem.at[0, j]),
            pltpu.make_async_copy(left.at[:, own + j], lkeep.at[:, j], keep_sem.at[1, j]),
        )
        for j in range(HT)
    ]
    queue = sends[:3]
    for j in range(3, HT):
        queue += [keeps[j - 3], sends[j]]
    queue += keeps[HT - 3 :]

    def begin(count):
        for _ in range(count):
            if queue:
                for copy in queue.pop(0):
                    copy.start()

    start_copy.start()
    begin(2)
    start_copy.wait()
    begin(1)
    acc = jnp.zeros((8, T), F32)
    for at in chunks():
        value = start[at, :]
        acc += fold(value * value)
    scale = lax.rsqrt(total(acc) / COUNT + 1e-6)
    for at in chunks():
        value = start[at, :] * scale
        state[at, :] = value
        store_split(vc, at.start, value)
    for j in range(HT):
        for copy in sends[j]:
            copy.wait()
        begin(2)
        prepare(lbuf, rbuf, j, lc, rc)
        send[j * T : (j + 1) * T, :] = tile_terms(other + j, j, table, vc, lc, rc)
    for pair in keeps:
        for copy in pair:
            copy.wait()


def offsets(info):
    own, other = info[0] * HALF, (1 - info[0]) * HALF
    places = [own + (info[1] ^ m) * PIECE for m in range(4)]
    places += [other + (info[2] ^ m) * PIECE for m in range(4)]
    return places


def next_direct(state, sigma_at, theta, diag, pre, direct, vc):
    acc = jnp.zeros((8, T), F32)
    for at in chunks():
        st, sg = sigma_at(at)
        away = diag[at, :] - theta
        value = (sg - theta * st) * lax.rsqrt(away * away + 1.0)
        pre[at, :] = value
        acc += fold(st * value)
    proj = total(acc) / COUNT
    acc = jnp.zeros((8, T), F32)
    for at in chunks():
        value = pre[at, :] - proj * state[at, :]
        pre[at, :] = value
        acc += fold(value * value)
    scale = lax.rsqrt(total(acc) / COUNT + 1e-6)
    for at in chunks():
        value = pre[at, :] * scale
        direct[at, :] = value
        store_split(vc, at.start, value)


def gathered(info, pieces, vector, other, diag, result):
    acc_v, acc_o = jnp.zeros((8, T), F32), jnp.zeros((8, T), F32)
    for i, begin in enumerate(offsets(info)):
        for here in chunks(PIECE):
            at = pl.ds(pl.multiple_of(begin + here.start, STEP), STEP)
            vec = vector[at, :]
            value = pieces[i // 4][pl.ds(i % 4 * PIECE + here.start, STEP), :] + diag[at, :] * vec
            result[at, :] = value
            acc_v += fold(vec * value)
            if other is not None:
                acc_o += fold(other[at, :] * value)
    return total(acc_v) / COUNT, total(acc_o) / COUNT


def rotation(theta, bval, cval):
    gap = (theta - bval) / 2.0
    root = jnp.sqrt(gap * gap + cval * cval)
    lam = (theta + bval) / 2.0 - root
    first = bval - lam
    inverse = lax.rsqrt(first * first + cval * cval + 1e-12)
    return lam, first * inverse, cval * inverse


def partial_products(state, direct, diag, table, vc, halves, terms, weights, scal):
    for which, lc, rc in halves:
        for j in range(HT):
            b = which * HT + j
            at = pl.ds(pl.multiple_of(b * T, T), T)
            terms[at, :] = tile_terms(b, j, table, vc, lc, rc)
    acc_b, acc_c = jnp.zeros((8, T), F32), jnp.zeros((8, T), F32)
    for at in chunks():
        vec = direct[at, :]
        value = terms[at, :] + (1.0 / 32) * (diag[at, :] * vec)
        acc_b += fold(vec * value)
        acc_c += fold(state[at, :] * value)
    scal[...] = jnp.zeros_like(scal)
    scal[0:1, :] = jnp.sum(acc_b, axis=0, keepdims=True)
    scal[1:2, :] = jnp.sum(acc_c, axis=0, keepdims=True)
    scal[4:8, 0:32] = weights[...]


def first_kernel(info, table, *refs):
    pieces, (state, diag, lc, rc, send, vc, sigma, direct, theta_out, pre) = refs[:2], refs[2:]
    theta, _ = gathered(info, pieces, state, None, diag, sigma)
    theta_out[...] = jnp.broadcast_to(theta, theta_out.shape)
    next_direct(state, lambda at: (state[at, :], sigma[at, :]), theta, diag, pre, direct, vc)
    half_terms(1 - info[0], table, vc, lc, rc, send)


def step_kernel(last, info, table, *refs):
    pieces, refs = refs[:2], refs[2:]
    state, sigma, direct, theta, diag, lc, rc = refs[:7]
    refs = refs[7:]
    if last:
        (lkeep, rkeep, weights), refs = refs[:3], refs[3:]
    out, vc, state_out, sigma_out, direct_out, theta_out, pre, hdirect = refs
    bval, cval = gathered(info, pieces, direct, state, diag, hdirect)
    lam, first, second = rotation(theta[0:1, 0:1], bval, cval)
    theta_out[...] = jnp.broadcast_to(lam, theta_out.shape)

    def updated(at):
        st = first * state[at, :] - second * direct[at, :]
        sg = first * sigma[at, :] - second * hdirect[at, :]
        state_out[at, :] = st
        sigma_out[at, :] = sg
        return st, sg

    next_direct(state_out, updated, lam, diag, pre, direct_out, vc)
    if last:
        halves = ((1 - info[0], lc, rc), (info[0], lkeep, rkeep))
        partial_products(state_out, direct_out, diag, table, vc, halves, pre, weights, out)
    else:
        half_terms(1 - info[0], table, vc, lc, rc, out)


VECTOR = shape(ROWS, T)
SPLIT = shape(NB, T, 2 * T, dtype=BF)
SCALAR = shape(8, T)


def call(kernel, name, n_smem, args, outs, scratch=(), flops=0, n_hbm=0, mib=24):
    n_vmem = len(args) - n_smem - n_hbm
    hbm = [pltpu.with_memory_space_constraint(arg, pltpu.HBM) for arg in args[n_smem + n_vmem :]]
    return pl.pallas_call(
        kernel,
        in_specs=[SMEM] * n_smem + [VMEM] * n_vmem + [HBM] * n_hbm,
        out_specs=[VMEM] * len(outs),
        out_shape=[pltpu.VMEM(out.shape, out.dtype) for out in outs],
        scratch_shapes=list(scratch),
        compiler_params=pltpu.CompilerParams(vmem_limit_bytes=mib << 20),
        cost_estimate=pl.CostEstimate(flops=flops, bytes_accessed=1 << 20, transcendentals=0),
        name=name,
    )(*args[: n_smem + n_vmem], *hbm)


def sum4(own, got):
    return (own + got[0]) + (got[2] + got[1])


def along(values, first):
    return [lax.ppermute(values[m], "op", line_pairs(m, first)) for m in (1, 3, 2)]


def cut(value, at, count):
    begin = [at] + [jnp.zeros_like(at)] * (value.ndim - 1)
    return lax.dynamic_slice(value, begin, (count, *value.shape[1:]), allow_negative_indices=False)


def sum_terms(begins, send, keep):
    got = lax.ppermute(send, "op", CORE_PAIRS)

    mine = [cut(keep, at, PIECE) + cut(got, at, PIECE) for at in begins]
    part = sum4(mine[0], along(mine, True))
    whole = sum4(part, along([part] * 4, False))
    got = along([whole] * 4, True)
    half = jnp.concatenate([whole, got[0], got[2], got[1]], axis=0)
    return half, lax.ppermute(half, "op", CORE_PAIRS)


def renorm_kernel(info, table, scal, state, direct, theta, lc, lkeep, rows, renorm, final, fc, ft, moved):
    acc = jnp.sum(scal[...], axis=0)
    bval = jnp.sum(acc[0:1, :], axis=1, keepdims=True) / COUNT
    cval = jnp.sum(acc[1:2, :], axis=1, keepdims=True) / COUNT
    _, first, second = rotation(theta[0:1, 0:1], bval, cval)
    for at in chunks():
        value = first * state[at, :] - second * direct[at, :]
        final[at, :] = value
        store_split(fc, at.start, value)
    rows[...] = final[pl.ds(pl.multiple_of(info[3], ROWS // 32), ROWS // 32), :]
    order = [((1 - info[0]) * HT + j, lc, j) for j in range(HT)] + [(info[0] * HT + j, lkeep, j) for j in range(HT)]
    for i, (b, ops, j) in enumerate(order):
        high, low = split(final[pl.ds(pl.multiple_of(b * T, T), T), :].T)
        ft[0:T, i * T : (i + 1) * T] = high
        ft[T : 2 * T, i * T : (i + 1) * T] = low
        for k in range(NK):
            at = pl.ds(k * T, T)
            lhs = jnp.concatenate([ops[j, 0:T, at], ops[j, T : 2 * T, at]], axis=1)
            picked = fc[table[k, b]]
            wide = dot(lhs, jnp.concatenate([picked, picked], axis=0))
            high, low = split(wide[:, :T] + wide[:, T:])
            moved[i * T : (i + 1) * T, 2 * k * T : (2 * k + 1) * T] = high
            moved[i * T : (i + 1) * T, (2 * k + 1) * T : (2 * k + 2) * T] = low
    for k in range(NK):
        wide = dot(ft[...], moved[:, 2 * k * T : (2 * k + 2) * T])
        renorm[k] = (wide[:T, :T] + (wide[:T, T:] + wide[T:, :T])) * (1.0 / T)


def newop_kernel(info, own_weights, other_scal, own, other, *outs):
    along_t = jnp.where(info[0] == 0, 4, 1)
    along_q = 5 - along_t
    for m, out in enumerate(outs):
        for t in range(4):
            j = 2 * (t * along_t + (info[1] ^ m) * along_q) + info[0]
            acc = None
            for k in range(NK):
                for weight, renorm in ((own_weights[k, j], own), (other_scal[4 + k, j], other)):
                    term = weight * renorm[k]
                    acc = term if acc is None else acc + term
            out[t] = acc


def per_device(start_state, diagonal, left_ops, right_ops, coupling, integrals):
    start, diag, table = start_state[0], diagonal[0], coupling[0]
    op = lax.axis_index("op")
    core, x, y = op % 2, (op // 2) % 4, op // 8
    quarter, other_quarter = jnp.where(core == 0, x, y), jnp.where(core == 0, y, x)
    chain = lax.axis_index("chain")
    info = jnp.stack([core, quarter, other_quarter, op * (ROWS // 32)]).astype(jnp.int32)
    begins = [(quarter ^ m) * PIECE for m in range(4)]
    positions = [other_quarter ^ m for m in range(4)]
    info, begins, positions, odd, upper, lower = lax.optimization_barrier(
        (info, begins, positions, chain % 2 > 0, chain % 4 > 1, chain < 4)
    )
    lc_shape = shape(HT, 2 * T, NK * T, dtype=BF)
    rc_shape = shape(HT, NK, T, 2 * T, dtype=BF)
    raw = (NK, HT, T, T)
    send, vc, state, lc, rc, lraw, rraw = call(
        start_kernel,
        "start",
        2,
        (info, table, start, left_ops[0], right_ops[0]),
        [shape(HALF, T), SPLIT, VECTOR, lc_shape, rc_shape, shape(*raw), shape(*raw)],
        [pltpu.VMEM((ROWS, T), F32), pltpu.VMEM(raw, F32), pltpu.VMEM(raw, F32)]
        + [pltpu.SemaphoreType.DMA, pltpu.SemaphoreType.DMA((2, HT)), pltpu.SemaphoreType.DMA((2, HT))],
        n_hbm=3,
    )
    keep, lkeep, rkeep = call(
        first_keep_kernel,
        "first_keep",
        2,
        (info, table, vc, lraw, rraw),
        [shape(HALF, T), lc_shape, rc_shape],
        flops=1 << 31,
    )
    pieces = sum_terms(begins, send, keep)
    send, vc, sigma, direct, theta = call(
        first_kernel,
        "first",
        2,
        (info, table, *pieces, state, diag, lc, rc),
        [shape(HALF, T), SPLIT, VECTOR, VECTOR, SCALAR],
        [pltpu.VMEM((ROWS, T), F32)],
    )
    for step in range(1, ITERS):
        keep = call(
            keep_kernel, "keep", 2, (info, table, vc, lkeep, rkeep), [shape(HALF, T)], flops=1 << 31
        )[0]
        pieces = sum_terms(begins, send, keep)
        last = step == ITERS - 1
        ops = (lc, rc, lkeep, rkeep, integrals) if last else (lc, rc)
        send, vc, state, sigma, direct, theta = call(
            functools.partial(step_kernel, last),
            "last" if last else "step",
            2,
            (info, table, *pieces, state, sigma, direct, theta, diag, *ops),
            [SCALAR if last else shape(HALF, T), SPLIT, VECTOR, VECTOR, VECTOR, SCALAR],
            [pltpu.VMEM((ROWS, T), F32)] * 2,
        )
    groups = [[2 * p + c for p in range(16)] for c in range(2)]
    other_scal = lax.ppermute(send, "op", CORE_PAIRS)
    scal = send + other_scal
    scal = lax.all_to_all(jnp.broadcast_to(scal[None], (16, 8, T)), "op", 0, 0, axis_index_groups=groups)
    own_rows, renorm = call(
        renorm_kernel,
        "renorm",
        2,
        (info, table, scal, state, direct, theta, lc, lkeep),
        [shape(ROWS // 32, T), shape(NK, T, T)],
        [
            pltpu.VMEM((ROWS, T), F32),
            pltpu.VMEM((NB, T, 2 * T), BF),
            pltpu.VMEM((2 * T, ROWS), BF),
            pltpu.VMEM((ROWS, 2 * NK * T), BF),
        ],
    )
    other = lax.ppermute(renorm, "op", CORE_PAIRS)
    newops = call(
        newop_kernel,
        "newops",
        3,
        (info, integrals, other_scal, renorm, other),
        [shape(4, T, T)] * 4,
    )
    got = [newops[0]] + along(newops, True)

    def position(at):
        mine, *others = [cut(value, at, 1)[0] for value in got]
        return sum4(mine, others)

    mine = [position(at) for at in positions]
    newop = sum4(mine[0], along(mine, False))
    got = lax.ppermute(newop, "chain", [(i, i ^ 1) for i in range(8)])
    before, pair = jnp.where(odd, got, 0.0), newop + got
    got = lax.ppermute(pair, "chain", [(i, i ^ 2) for i in range(8)])
    before, four = before + jnp.where(upper, got, 0.0), pair + got
    got = lax.ppermute(four, "chain", [(0, 6), (1, 7), (2, 4), (3, 5), (6, 0), (7, 1), (4, 2), (5, 3)])
    environment = newop + before + jnp.where(lower, 0.0, got)
    return (own_rows[None], environment[None, None])


def solution(mesh):
    placed = (
        P("chain", None, None),
        P("chain", None, None),
        P("chain", "op", None, None, None),
        P("chain", "op", None, None, None),
        P("chain", "op", None),
        P("op", None),
    )
    return jax.shard_map(
        per_device,
        mesh=mesh,
        in_specs=placed,
        out_specs=(P("chain", "op", None), P("chain", "op", None, None)),
        check_vma=False,
    )
```

```python
import functools

import jax
import jax.numpy as jnp
from jax import lax
from jax.experimental import pallas as pl
from jax.experimental.pallas import tpu as pltpu
from jax.sharding import PartitionSpec as P

ITERS = 4
T = 128
NB = 16
NK = 4
ROWS = NB * T
HALF = ROWS // 2
HT = NB // 2
PIECE = HALF // 4
COUNT = float(ROWS * T)
BF = jnp.bfloat16
F32 = jnp.float32
VMEM = pl.BlockSpec(memory_space=pltpu.VMEM)
HBM = pl.BlockSpec(memory_space=pltpu.HBM)
SMEM = pl.BlockSpec(memory_space=pltpu.SMEM)


def shape(*dims, dtype=F32):
    return jax.ShapeDtypeStruct(dims, dtype)


def place(y, x, c):
    return (y * 4 + x) * 2 + c


def line_pairs(m, first):
    pairs = []
    for y in range(4):
        for x in range(4):
            for c in range(2):
                along_x = (c == 0) == first
                to = place(y, x ^ m, c) if along_x else place(y ^ m, x, c)
                pairs.append((place(y, x, c), to))
    return pairs


CORE_PAIRS = [(i, i ^ 1) for i in range(32)]


def split(value):
    high = value.astype(BF)
    low = (value - high.astype(F32)).astype(BF)
    return high, low


def dot(a, b):
    return jnp.dot(a, b, preferred_element_type=F32)


def total(acc):
    return jnp.sum(jnp.sum(acc, axis=0, keepdims=True), axis=1, keepdims=True)


def fold(value):
    return jnp.sum(value.reshape(-1, 8, T), axis=0)


STEP = 64


def chunks(rows=ROWS):
    return [pl.ds(i, STEP) for i in range(0, rows, STEP)]


def prepare(left, right, j, lc, rc):
    for k in range(NK):
        high, low = split(left[k, j])
        lc[j, 0:T, k * T : (k + 1) * T] = high
        lc[j, T : 2 * T, k * T : (k + 1) * T] = low
        high, low = split(right[k, j].T)
        rc[j, k, :, 0:T] = high
        rc[j, k, :, T : 2 * T] = low


def tile_inner(b, j, table, vc, rc):
    parts = []
    for k in range(NK):
        picked = vc[table[k, b]]
        weights = jnp.concatenate([rc[j, k], rc[j, k]], axis=0)
        wide = dot(picked, weights)
        parts.append(jnp.concatenate(split(wide[:, :T] + wide[:, T:]), axis=1))
    return jnp.concatenate(parts, axis=0)


def tile_outer(j, lc, inner):
    wide = dot(lc[j], inner)
    return wide[:T, :T] + (wide[:T, T:] + wide[T:, :T])


def half_terms(which, table, vc, lc, rc, out, scale=None, between=None):
    inner = tile_inner(which * HT, 0, table, vc, rc)
    for j in range(HT):
        later = tile_inner(which * HT + j + 1, j + 1, table, vc, rc) if j + 1 < HT else None
        value = tile_outer(j, lc, inner)
        inner = later
        out[j * T : (j + 1) * T, :] = value if scale is None else value * scale
        if between is not None:
            between(j, HT)


def store_split(vc, row, value):
    high, low = split(value)
    at = pl.ds(row % T, STEP)
    vc[row // T, at, 0:T] = high
    vc[row // T, at, T : 2 * T] = low


def keep_kernel(info, table, vc, scale, lc, rc, out):
    half_terms(info[0], table, vc, lc, rc, out, scale[0:1, 0:1])


def first_keep_kernel(info, table, vc, left, right, out, lc, rc):
    prepare(left, right, 0, lc, rc)
    inner = tile_inner(info[0] * HT, 0, table, vc, rc)
    for j in range(HT):
        later = None
        if j + 1 < HT:
            prepare(left, right, j + 1, lc, rc)
            later = tile_inner(info[0] * HT + j + 1, j + 1, table, vc, rc)
        out[j * T : (j + 1) * T, :] = tile_outer(j, lc, inner)
        inner = later


def start_kernel(
    info, table, start_hbm, left, right, send, vc, state, lc, rc, lkeep, rkeep, start, lbuf, rbuf, start_sem, sem, keep_sem
):
    own, other = info[0] * HT, (1 - info[0]) * HT
    start_copy = pltpu.make_async_copy(start_hbm, start, start_sem)
    sends = [
        (
            pltpu.make_async_copy(right.at[:, other + j], rbuf.at[:, j], sem.at[0, j]),
            pltpu.make_async_copy(left.at[:, other + j], lbuf.at[:, j], sem.at[1, j]),
        )
        for j in range(HT)
    ]
    keeps = [
        (
            pltpu.make_async_copy(right.at[:, own + j], rkeep.at[:, j], keep_sem.at[0, j]),
            pltpu.make_async_copy(left.at[:, own + j], lkeep.at[:, j], keep_sem.at[1, j]),
        )
        for j in range(HT)
    ]
    queue = sends[:3]
    for j in range(3, HT):
        queue += [keeps[j - 3], sends[j]]
    queue += keeps[HT - 3 :]

    def begin(count):
        for _ in range(count):
            if queue:
                for copy in queue.pop(0):
                    copy.start()

    def ready(j):
        if j < HT:
            for copy in sends[j]:
                copy.wait()
            begin(2)
            prepare(lbuf, rbuf, j, lc, rc)

    begin(1)
    start_copy.start()
    begin(2)
    ready(0)
    ready(1)
    start_copy.wait()
    acc = jnp.zeros((8, T), F32)
    for at in chunks():
        value = start[at, :]
        acc += fold(value * value)
    scale = lax.rsqrt(total(acc) / COUNT + 1e-6)
    for at in chunks():
        value = start[at, :] * scale
        state[at, :] = value
        store_split(vc, at.start, value)
    inner = tile_inner(other, 0, table, vc, rc)
    for j in range(HT):
        ready(j + 2)
        later = tile_inner(other + j + 1, j + 1, table, vc, rc) if j + 1 < HT else None
        send[j * T : (j + 1) * T, :] = tile_outer(j, lc, inner)
        inner = later
    for pair in keeps:
        for copy in pair:
            copy.wait()


def offsets(info):
    own, other = info[0] * HALF, (1 - info[0]) * HALF
    places = [own + (info[1] ^ m) * PIECE for m in (0, 1, 3, 2)]
    places += [other + (info[2] ^ m) * PIECE for m in (0, 1, 3, 2)]
    return places


def next_direct(state, sigma_at, theta, diag, pre, direct, vc):
    acc = jnp.zeros((8, T), F32)
    for at in chunks():
        st, sg = sigma_at(at)
        away = diag[at, :] - theta
        value = (sg - theta * st) * lax.rsqrt(away * away + 1.0)
        pre[at, :] = value
        acc += fold(st * value)
    proj = total(acc) / COUNT
    acc = jnp.zeros((8, T), F32)
    for at in chunks():
        value = pre[at, :] - proj * state[at, :]
        pre[at, :] = value
        store_split(vc, at.start, value)
        acc += fold(value * value)
    scale = lax.rsqrt(total(acc) / COUNT + 1e-6)

    def store(i, count):
        every = chunks()
        for at in every[i * len(every) // count : (i + 1) * len(every) // count]:
            direct[at, :] = pre[at, :] * scale

    return scale, store


def gathered(info, pieces, vector, other, diag, result):
    acc_v, acc_o = jnp.zeros((8, T), F32), jnp.zeros((8, T), F32)
    parts = [(pieces[i // 4], i % 4 * PIECE) for i in range(8)]
    for (piece, skip), begin in zip(parts, offsets(info), strict=True):
        for here in chunks(PIECE):
            at = pl.ds(pl.multiple_of(begin + here.start, STEP), STEP)
            vec = vector[at, :]
            value = piece[pl.ds(skip + here.start, STEP), :] + diag[at, :] * vec
            result[at, :] = value
            acc_v += fold(vec * value)
            if other is not None:
                acc_o += fold(other[at, :] * value)
    return total(acc_v) / COUNT, total(acc_o) / COUNT


def rotation(theta, bval, cval):
    gap = (theta - bval) / 2.0
    root = jnp.sqrt(gap * gap + cval * cval)
    lam = (theta + bval) / 2.0 - root
    first = bval - lam
    inverse = lax.rsqrt(first * first + cval * cval + 1e-12)
    return lam, first * inverse, cval * inverse


def partial_products(state, direct, diag, table, vc, halves, terms, weights, scal, scale, store):
    tiles = [(which * HT + j, j, lc, rc) for which, lc, rc in halves for j in range(HT)]
    b, j, lc, rc = tiles[0]
    inner = tile_inner(b, j, table, vc, rc)
    for i, (b, j, lc, rc) in enumerate(tiles):
        later = None
        if i + 1 < NB:
            next_b, next_j, _, next_rc = tiles[i + 1]
            later = tile_inner(next_b, next_j, table, vc, next_rc)
        at = pl.ds(pl.multiple_of(b * T, T), T)
        terms[at, :] = tile_outer(j, lc, inner) * scale
        inner = later
        store(i, NB)
    acc_b, acc_c = jnp.zeros((8, T), F32), jnp.zeros((8, T), F32)
    for at in chunks():
        vec = direct[at, :]
        value = terms[at, :] + (1.0 / 32) * (diag[at, :] * vec)
        acc_b += fold(vec * value)
        acc_c += fold(state[at, :] * value)
    scal[...] = jnp.zeros_like(scal)
    scal[0:1, :] = jnp.sum(acc_b, axis=0, keepdims=True)
    scal[1:2, :] = jnp.sum(acc_c, axis=0, keepdims=True)
    scal[4:8, 0:32] = weights[...]


def first_kernel(info, table, *refs):
    pieces, (state, diag, lc, rc, send, vc, sigma, direct, theta_out, scale_out, pre) = refs[:2], refs[2:]
    theta, _ = gathered(info, pieces, state, None, diag, sigma)
    theta_out[...] = jnp.broadcast_to(theta, theta_out.shape)
    scale, store = next_direct(state, lambda at: (state[at, :], sigma[at, :]), theta, diag, pre, direct, vc)
    scale_out[...] = jnp.broadcast_to(scale, scale_out.shape)
    half_terms(1 - info[0], table, vc, lc, rc, send, scale, store)


def step_kernel(last, info, table, *refs):
    pieces, refs = refs[:2], refs[2:]
    state, sigma, direct, theta, diag, lc, rc = refs[:7]
    refs = refs[7:]
    if last:
        (lkeep, rkeep, weights), refs = refs[:3], refs[3:]
    out, vc, state_out, sigma_out, direct_out, theta_out, scale_out, pre, hdirect, terms = refs
    bval, cval = gathered(info, pieces, direct, state, diag, hdirect)
    lam, first, second = rotation(theta[0:1, 0:1], bval, cval)
    theta_out[...] = jnp.broadcast_to(lam, theta_out.shape)

    def updated(at):
        st = first * state[at, :] - second * direct[at, :]
        sg = first * sigma[at, :] - second * hdirect[at, :]
        state_out[at, :] = st
        sigma_out[at, :] = sg
        return st, sg

    scale, store = next_direct(state_out, updated, lam, diag, pre, direct_out, vc)
    scale_out[...] = jnp.broadcast_to(scale, scale_out.shape)
    if last:
        halves = ((1 - info[0], lc, rc), (info[0], lkeep, rkeep))
        partial_products(state_out, direct_out, diag, table, vc, halves, terms, weights, out, scale, store)
    else:
        half_terms(1 - info[0], table, vc, lc, rc, out, scale, store)


VECTOR = shape(ROWS, T)
SPLIT = shape(NB, T, 2 * T, dtype=BF)
SCALAR = shape(8, T)


def call(kernel, name, n_smem, args, outs, scratch=(), flops=0, n_hbm=0, mib=24):
    n_vmem = len(args) - n_smem - n_hbm
    hbm = [pltpu.with_memory_space_constraint(arg, pltpu.HBM) for arg in args[n_smem + n_vmem :]]
    return pl.pallas_call(
        kernel,
        in_specs=[SMEM] * n_smem + [VMEM] * n_vmem + [HBM] * n_hbm,
        out_specs=[VMEM] * len(outs),
        out_shape=[pltpu.VMEM(out.shape, out.dtype) for out in outs],
        scratch_shapes=list(scratch),
        compiler_params=pltpu.CompilerParams(vmem_limit_bytes=mib << 20),
        cost_estimate=pl.CostEstimate(flops=flops, bytes_accessed=1 << 20, transcendentals=0),
        name=name,
    )(*args[: n_smem + n_vmem], *hbm)


def sum4(own, got):
    return (own + got[0]) + (got[2] + got[1])


def along(values, first):
    return [lax.ppermute(values[m], "op", line_pairs(m, first)) for m in (1, 3, 2)]


def cut(value, at, count):
    begin = [at] + [jnp.zeros_like(at)] * (value.ndim - 1)
    return lax.dynamic_slice(value, begin, (count, *value.shape[1:]), allow_negative_indices=False)


def sum_terms(begins, send, keep):
    got = lax.ppermute(send, "op", CORE_PAIRS)

    mine = [cut(keep, at, PIECE) + cut(got, at, PIECE) for at in begins]
    part = sum4(mine[0], along(mine, True))
    whole = sum4(part, along([part] * 4, False))
    got = along([whole] * 4, True)
    half = jnp.concatenate([whole, *got], axis=0)
    return half, lax.ppermute(half, "op", CORE_PAIRS)


def renorm_kernel(info, table, scal, state, direct, theta, lc, lkeep, rows, renorm, final, fc, ft, moved):
    acc = jnp.sum(scal[...], axis=0)
    bval = jnp.sum(acc[0:1, :], axis=1, keepdims=True) / COUNT
    cval = jnp.sum(acc[1:2, :], axis=1, keepdims=True) / COUNT
    _, first, second = rotation(theta[0:1, 0:1], bval, cval)
    for at in chunks():
        value = first * state[at, :] - second * direct[at, :]
        final[at, :] = value
        store_split(fc, at.start, value)
    rows[...] = final[pl.ds(pl.multiple_of(info[3], ROWS // 32), ROWS // 32), :]
    order = [((1 - info[0]) * HT + j, lc, j) for j in range(HT)] + [(info[0] * HT + j, lkeep, j) for j in range(HT)]
    for i, (b, ops, j) in enumerate(order):
        high, low = split(final[pl.ds(pl.multiple_of(b * T, T), T), :].T)
        ft[0:T, i * T : (i + 1) * T] = high
        ft[T : 2 * T, i * T : (i + 1) * T] = low
        for k in range(NK):
            at = pl.ds(k * T, T)
            lhs = jnp.concatenate([ops[j, 0:T, at], ops[j, T : 2 * T, at]], axis=1)
            picked = fc[table[k, b]]
            wide = dot(lhs, jnp.concatenate([picked, picked], axis=0))
            high, low = split(wide[:, :T] + wide[:, T:])
            moved[i * T : (i + 1) * T, 2 * k * T : (2 * k + 1) * T] = high
            moved[i * T : (i + 1) * T, (2 * k + 1) * T : (2 * k + 2) * T] = low
    for k in range(NK):
        wide = dot(ft[...], moved[:, 2 * k * T : (2 * k + 2) * T])
        renorm[k] = (wide[:T, :T] + (wide[:T, T:] + wide[T:, :T])) * (1.0 / T)


def newop_kernel(info, own_weights, other_scal, own, other, *outs):
    along_t = jnp.where(info[0] == 0, 4, 1)
    along_q = 5 - along_t
    for m, out in enumerate(outs):
        for t in range(4):
            j = 2 * (t * along_t + (info[1] ^ m) * along_q) + info[0]
            acc = None
            for k in range(NK):
                for weight, renorm in ((own_weights[k, j], own), (other_scal[4 + k, j], other)):
                    term = weight * renorm[k]
                    acc = term if acc is None else acc + term
            out[t] = acc


def per_device(start_state, diagonal, left_ops, right_ops, coupling, integrals):
    start, diag, table = start_state[0], diagonal[0], coupling[0]
    op = lax.axis_index("op")
    core, x, y = op % 2, (op // 2) % 4, op // 8
    quarter, other_quarter = jnp.where(core == 0, x, y), jnp.where(core == 0, y, x)
    chain = lax.axis_index("chain")
    info = jnp.stack([core, quarter, other_quarter, op * (ROWS // 32)]).astype(jnp.int32)
    begins = [(quarter ^ m) * PIECE for m in range(4)]
    positions = [other_quarter ^ m for m in range(4)]
    info, begins, positions, odd, upper, lower = lax.optimization_barrier(
        (info, begins, positions, chain % 2 > 0, chain % 4 > 1, chain < 4)
    )
    lc_shape = shape(HT, 2 * T, NK * T, dtype=BF)
    rc_shape = shape(HT, NK, T, 2 * T, dtype=BF)
    raw = (NK, HT, T, T)
    send, vc, state, lc, rc, lraw, rraw = call(
        start_kernel,
        "start",
        2,
        (info, table, start, left_ops[0], right_ops[0]),
        [shape(HALF, T), SPLIT, VECTOR, lc_shape, rc_shape, shape(*raw), shape(*raw)],
        [pltpu.VMEM((ROWS, T), F32), pltpu.VMEM(raw, F32), pltpu.VMEM(raw, F32)]
        + [pltpu.SemaphoreType.DMA, pltpu.SemaphoreType.DMA((2, HT)), pltpu.SemaphoreType.DMA((2, HT))],
        n_hbm=3,
    )
    keep, lkeep, rkeep = call(
        first_keep_kernel,
        "first_keep",
        2,
        (info, table, vc, lraw, rraw),
        [shape(HALF, T), lc_shape, rc_shape],
        flops=1 << 31,
    )
    pieces = sum_terms(begins, send, keep)
    send, vc, sigma, direct, theta, scale = call(
        first_kernel,
        "first",
        2,
        (info, table, *pieces, state, diag, lc, rc),
        [shape(HALF, T), SPLIT, VECTOR, VECTOR, SCALAR, SCALAR],
        [pltpu.VMEM((ROWS, T), F32)],
    )
    for step in range(1, ITERS):
        keep = call(
            keep_kernel, "keep", 2, (info, table, vc, scale, lkeep, rkeep), [shape(HALF, T)], flops=1 << 31
        )[0]
        pieces = sum_terms(begins, send, keep)
        last = step == ITERS - 1
        ops = (lc, rc, lkeep, rkeep, integrals) if last else (lc, rc)
        send, vc, state, sigma, direct, theta, scale = call(
            functools.partial(step_kernel, last),
            "last" if last else "step",
            2,
            (info, table, *pieces, state, sigma, direct, theta, diag, *ops),
            [SCALAR if last else shape(HALF, T), SPLIT, VECTOR, VECTOR, VECTOR, SCALAR, SCALAR],
            [pltpu.VMEM((ROWS, T), F32)] * 3,
        )
    groups = [[2 * p + c for p in range(16)] for c in range(2)]
    other_scal = lax.ppermute(send, "op", CORE_PAIRS)
    scal = send + other_scal
    scal = lax.all_to_all(jnp.broadcast_to(scal[None], (16, 8, T)), "op", 0, 0, axis_index_groups=groups)
    own_rows, renorm = call(
        renorm_kernel,
        "renorm",
        2,
        (info, table, scal, state, direct, theta, lc, lkeep),
        [shape(ROWS // 32, T), shape(NK, T, T)],
        [
            pltpu.VMEM((ROWS, T), F32),
            pltpu.VMEM((NB, T, 2 * T), BF),
            pltpu.VMEM((2 * T, ROWS), BF),
            pltpu.VMEM((ROWS, 2 * NK * T), BF),
        ],
    )
    other = lax.ppermute(renorm, "op", CORE_PAIRS)
    newops = call(
        newop_kernel,
        "newops",
        3,
        (info, integrals, other_scal, renorm, other),
        [shape(4, T, T)] * 4,
    )
    got = [newops[0]] + along(newops, True)

    def position(at):
        mine, *others = [cut(value, at, 1)[0] for value in got]
        return sum4(mine, others)

    mine = [position(at) for at in positions]
    newop = sum4(mine[0], along(mine, False))
    got = lax.ppermute(newop, "chain", [(i, i ^ 1) for i in range(8)])
    before, pair = jnp.where(odd, got, 0.0), newop + got
    got = lax.ppermute(pair, "chain", [(i, i ^ 2) for i in range(8)])
    before, four = before + jnp.where(upper, got, 0.0), pair + got
    got = lax.ppermute(four, "chain", [(0, 6), (1, 7), (2, 4), (3, 5), (6, 0), (7, 1), (4, 2), (5, 3)])
    environment = newop + before + jnp.where(lower, 0.0, got)
    return (own_rows[None], environment[None, None])


def solution(mesh):
    placed = (
        P("chain", None, None),
        P("chain", None, None),
        P("chain", "op", None, None, None),
        P("chain", "op", None, None, None),
        P("chain", "op", None),
        P("op", None),
    )
    return jax.shard_map(
        per_device,
        mesh=mesh,
        in_specs=placed,
        out_specs=(P("chain", "op", None), P("chain", "op", None, None)),
        check_vma=False,
    )
```

```python
import functools

import jax
import jax.numpy as jnp
from jax import lax
from jax.experimental import pallas as pl
from jax.experimental.pallas import tpu as pltpu
from jax.sharding import PartitionSpec as P

ITERS = 4
T = 128
NB = 16
NK = 4
ROWS = NB * T
HALF = ROWS // 2
HT = NB // 2
PIECE = HALF // 4
COUNT = float(ROWS * T)
BF = jnp.bfloat16
F32 = jnp.float32
VMEM = pl.BlockSpec(memory_space=pltpu.VMEM)
HBM = pl.BlockSpec(memory_space=pltpu.HBM)
SMEM = pl.BlockSpec(memory_space=pltpu.SMEM)


def shape(*dims, dtype=F32):
    return jax.ShapeDtypeStruct(dims, dtype)


def place(y, x, c):
    return (y * 4 + x) * 2 + c


def line_pairs(m, first):
    pairs = []
    for y in range(4):
        for x in range(4):
            for c in range(2):
                along_x = (c == 0) == first
                to = place(y, x ^ m, c) if along_x else place(y ^ m, x, c)
                pairs.append((place(y, x, c), to))
    return pairs


CORE_PAIRS = [(i, i ^ 1) for i in range(32)]


def split(value):
    high = value.astype(BF)
    low = (value - high.astype(F32)).astype(BF)
    return high, low


def dot(a, b):
    return jnp.dot(a, b, preferred_element_type=F32)


def total(acc):
    return jnp.sum(jnp.sum(acc, axis=0, keepdims=True), axis=1, keepdims=True)


def fold(value):
    return jnp.sum(value.reshape(-1, 8, T), axis=0)


STEP = 64


def chunks(rows=ROWS):
    return [pl.ds(i, STEP) for i in range(0, rows, STEP)]


def prepare(left, right, j, lc, rc):
    for k in range(NK):
        high, low = split(left[k, j])
        lc[j, 0:T, k * T : (k + 1) * T] = high
        lc[j, T : 2 * T, k * T : (k + 1) * T] = low
        high, low = split(right[k, j].T)
        rc[j, k, :, 0:T] = high
        rc[j, k, :, T : 2 * T] = low


def tile_inner(b, j, table, vc, rc):
    parts = []
    for k in range(NK):
        picked = vc[table[k, b]]
        weights = jnp.concatenate([rc[j, k], rc[j, k]], axis=0)
        wide = dot(picked, weights)
        parts.append(jnp.concatenate(split(wide[:, :T] + wide[:, T:]), axis=1))
    return jnp.concatenate(parts, axis=0)


def tile_outer(j, lc, inner):
    wide = dot(lc[j], inner)
    return wide[:T, :T] + (wide[:T, T:] + wide[T:, :T])


def half_terms(which, table, vc, lc, rc, out, scale=None, between=None):
    inner = tile_inner(which * HT, 0, table, vc, rc)
    for j in range(HT):
        later = tile_inner(which * HT + j + 1, j + 1, table, vc, rc) if j + 1 < HT else None
        value = tile_outer(j, lc, inner)
        inner = later
        out[j * T : (j + 1) * T, :] = value if scale is None else value * scale
        if between is not None:
            between(j, HT)


def store_split(vc, row, value):
    high, low = split(value)
    at = pl.ds(row % T, STEP)
    vc[row // T, at, 0:T] = high
    vc[row // T, at, T : 2 * T] = low


def keep_kernel(info, table, vc, scale, lc, rc, out):
    half_terms(info[0], table, vc, lc, rc, out, scale[0:1, 0:1])


def first_keep_kernel(info, table, vc, left, right, out, lc, rc):
    prepare(left, right, 0, lc, rc)
    inner = tile_inner(info[0] * HT, 0, table, vc, rc)
    for j in range(HT):
        later = None
        if j + 1 < HT:
            prepare(left, right, j + 1, lc, rc)
            later = tile_inner(info[0] * HT + j + 1, j + 1, table, vc, rc)
        out[j * T : (j + 1) * T, :] = tile_outer(j, lc, inner)
        inner = later


def start_kernel(
    info, table, start_hbm, left, right, send, vc, state, lc, rc, lkeep, rkeep, start, lbuf, rbuf, start_sem, sem, keep_sem
):
    own, other = info[0] * HT, (1 - info[0]) * HT
    start_copy = pltpu.make_async_copy(start_hbm, start, start_sem)
    sends = [
        (
            pltpu.make_async_copy(right.at[:, other + j], rbuf.at[:, j], sem.at[0, j]),
            pltpu.make_async_copy(left.at[:, other + j], lbuf.at[:, j], sem.at[1, j]),
        )
        for j in range(HT)
    ]
    keeps = [
        (
            pltpu.make_async_copy(right.at[:, own + j], rkeep.at[:, j], keep_sem.at[0, j]),
            pltpu.make_async_copy(left.at[:, own + j], lkeep.at[:, j], keep_sem.at[1, j]),
        )
        for j in range(HT)
    ]
    queue = sends[:3]
    for j in range(3, HT):
        queue += [keeps[j - 3], sends[j]]
    queue += keeps[HT - 3 :]

    def begin(count):
        for _ in range(count):
            if queue:
                for copy in queue.pop(0):
                    copy.start()

    def ready(j):
        if j < HT:
            for copy in sends[j]:
                copy.wait()
            begin(2)
            prepare(lbuf, rbuf, j, lc, rc)

    begin(1)
    start_copy.start()
    begin(2)
    ready(0)
    ready(1)
    start_copy.wait()
    acc = jnp.zeros((8, T), F32)
    for at in chunks():
        value = start[at, :]
        acc += fold(value * value)
    scale = lax.rsqrt(total(acc) / COUNT + 1e-6)
    for at in chunks():
        value = start[at, :] * scale
        state[at, :] = value
        store_split(vc, at.start, value)
    inner = tile_inner(other, 0, table, vc, rc)
    for j in range(HT):
        ready(j + 2)
        later = tile_inner(other + j + 1, j + 1, table, vc, rc) if j + 1 < HT else None
        send[j * T : (j + 1) * T, :] = tile_outer(j, lc, inner)
        inner = later
    for pair in keeps:
        for copy in pair:
            copy.wait()


def offsets(info):
    own, other = info[0] * HALF, (1 - info[0]) * HALF
    places = [own + (info[1] ^ m) * PIECE for m in (0, 1, 3, 2)]
    places += [other + (info[2] ^ m) * PIECE for m in (0, 1, 3, 2)]
    return places


def next_direct(state, sigma_at, theta, diag, pre, direct, vc):
    acc = jnp.zeros((8, T), F32)
    for at in chunks():
        st, sg = sigma_at(at)
        away = diag[at, :] - theta
        value = (sg - theta * st) * lax.rsqrt(away * away + 1.0)
        pre[at, :] = value
        acc += fold(st * value)
    proj = total(acc) / COUNT
    acc = jnp.zeros((8, T), F32)
    for at in chunks():
        value = pre[at, :] - proj * state[at, :]
        pre[at, :] = value
        store_split(vc, at.start, value)
        acc += fold(value * value)
    scale = lax.rsqrt(total(acc) / COUNT + 1e-6)

    def store(i, count):
        every = chunks()
        for at in every[i * len(every) // count : (i + 1) * len(every) // count]:
            direct[at, :] = pre[at, :] * scale

    return scale, store


def gathered(info, pieces, vector, other, diag, result):
    acc_v, acc_o = jnp.zeros((8, T), F32), jnp.zeros((8, T), F32)
    for piece, begin in zip(pieces, offsets(info), strict=True):
        for here in chunks(PIECE):
            at = pl.ds(pl.multiple_of(begin + here.start, STEP), STEP)
            vec = vector[at, :]
            value = piece[here, :] + diag[at, :] * vec
            result[at, :] = value
            acc_v += fold(vec * value)
            if other is not None:
                acc_o += fold(other[at, :] * value)
    return total(acc_v) / COUNT, total(acc_o) / COUNT


def rotation(theta, bval, cval):
    gap = (theta - bval) / 2.0
    root = jnp.sqrt(gap * gap + cval * cval)
    lam = (theta + bval) / 2.0 - root
    first = bval - lam
    inverse = lax.rsqrt(first * first + cval * cval + 1e-12)
    return lam, first * inverse, cval * inverse


def partial_products(state, direct, diag, table, vc, halves, terms, weights, scal, scale, store):
    tiles = [(which * HT + j, j, lc, rc) for which, lc, rc in halves for j in range(HT)]
    b, j, lc, rc = tiles[0]
    inner = tile_inner(b, j, table, vc, rc)
    for i, (b, j, lc, rc) in enumerate(tiles):
        later = None
        if i + 1 < NB:
            next_b, next_j, _, next_rc = tiles[i + 1]
            later = tile_inner(next_b, next_j, table, vc, next_rc)
        at = pl.ds(pl.multiple_of(b * T, T), T)
        terms[at, :] = tile_outer(j, lc, inner) * scale
        inner = later
        store(i, NB)
    acc_b, acc_c = jnp.zeros((8, T), F32), jnp.zeros((8, T), F32)
    for at in chunks():
        vec = direct[at, :]
        value = terms[at, :] + (1.0 / 32) * (diag[at, :] * vec)
        acc_b += fold(vec * value)
        acc_c += fold(state[at, :] * value)
    scal[...] = jnp.zeros_like(scal)
    scal[0:1, :] = jnp.sum(acc_b, axis=0, keepdims=True)
    scal[1:2, :] = jnp.sum(acc_c, axis=0, keepdims=True)
    scal[4:8, 0:32] = weights[...]


def first_kernel(info, table, *refs):
    pieces, (state, diag, lc, rc, send, vc, sigma, direct, theta_out, scale_out, pre) = refs[:8], refs[8:]
    theta, _ = gathered(info, pieces, state, None, diag, sigma)
    theta_out[...] = jnp.broadcast_to(theta, theta_out.shape)
    scale, store = next_direct(state, lambda at: (state[at, :], sigma[at, :]), theta, diag, pre, direct, vc)
    scale_out[...] = jnp.broadcast_to(scale, scale_out.shape)
    half_terms(1 - info[0], table, vc, lc, rc, send, scale, store)


def step_kernel(last, info, table, *refs):
    pieces, refs = refs[:8], refs[8:]
    state, sigma, direct, theta, diag, lc, rc = refs[:7]
    refs = refs[7:]
    if last:
        (lkeep, rkeep, weights), refs = refs[:3], refs[3:]
    out, vc, state_out, sigma_out, direct_out, theta_out, scale_out, pre, hdirect, terms = refs
    bval, cval = gathered(info, pieces, direct, state, diag, hdirect)
    lam, first, second = rotation(theta[0:1, 0:1], bval, cval)
    theta_out[...] = jnp.broadcast_to(lam, theta_out.shape)

    def updated(at):
        st = first * state[at, :] - second * direct[at, :]
        sg = first * sigma[at, :] - second * hdirect[at, :]
        state_out[at, :] = st
        sigma_out[at, :] = sg
        return st, sg

    scale, store = next_direct(state_out, updated, lam, diag, pre, direct_out, vc)
    scale_out[...] = jnp.broadcast_to(scale, scale_out.shape)
    if last:
        halves = ((1 - info[0], lc, rc), (info[0], lkeep, rkeep))
        partial_products(state_out, direct_out, diag, table, vc, halves, terms, weights, out, scale, store)
    else:
        half_terms(1 - info[0], table, vc, lc, rc, out, scale, store)


VECTOR = shape(ROWS, T)
SPLIT = shape(NB, T, 2 * T, dtype=BF)
SCALAR = shape(8, T)


def call(kernel, name, n_smem, args, outs, scratch=(), flops=0, n_hbm=0, mib=24):
    n_vmem = len(args) - n_smem - n_hbm
    hbm = [pltpu.with_memory_space_constraint(arg, pltpu.HBM) for arg in args[n_smem + n_vmem :]]
    return pl.pallas_call(
        kernel,
        in_specs=[SMEM] * n_smem + [VMEM] * n_vmem + [HBM] * n_hbm,
        out_specs=[VMEM] * len(outs),
        out_shape=[pltpu.VMEM(out.shape, out.dtype) for out in outs],
        scratch_shapes=list(scratch),
        compiler_params=pltpu.CompilerParams(vmem_limit_bytes=mib << 20),
        cost_estimate=pl.CostEstimate(flops=flops, bytes_accessed=1 << 20, transcendentals=0),
        name=name,
    )(*args[: n_smem + n_vmem], *hbm)


def sum4(own, got):
    return (own + got[0]) + (got[2] + got[1])


def along(values, first):
    return [lax.ppermute(values[m], "op", line_pairs(m, first)) for m in (1, 3, 2)]


def cut(value, at, count):
    begin = [at] + [jnp.zeros_like(at)] * (value.ndim - 1)
    return lax.dynamic_slice(value, begin, (count, *value.shape[1:]), allow_negative_indices=False)


def sum_terms(begins, send, keep):
    got = lax.ppermute(send, "op", CORE_PAIRS)

    mine = [cut(keep, at, PIECE) + cut(got, at, PIECE) for at in begins]
    part = sum4(mine[0], along(mine, True))
    whole = sum4(part, along([part] * 4, False))
    far, last, near = [lax.ppermute(whole, "op", line_pairs(m, True)) for m in (2, 3, 1)]
    own = [whole, near, last, far]
    return own + [lax.ppermute(value, "op", CORE_PAIRS) for value in own]


def renorm_kernel(info, table, scal, state, direct, theta, lc, lkeep, rows, renorm, final, fc, ft, moved):
    acc = jnp.sum(scal[...], axis=0)
    bval = jnp.sum(acc[0:1, :], axis=1, keepdims=True) / COUNT
    cval = jnp.sum(acc[1:2, :], axis=1, keepdims=True) / COUNT
    _, first, second = rotation(theta[0:1, 0:1], bval, cval)
    for at in chunks():
        value = first * state[at, :] - second * direct[at, :]
        final[at, :] = value
        store_split(fc, at.start, value)
    rows[...] = final[pl.ds(pl.multiple_of(info[3], ROWS // 32), ROWS // 32), :]
    order = [((1 - info[0]) * HT + j, lc, j) for j in range(HT)] + [(info[0] * HT + j, lkeep, j) for j in range(HT)]
    for i, (b, ops, j) in enumerate(order):
        high, low = split(final[pl.ds(pl.multiple_of(b * T, T), T), :].T)
        ft[0:T, i * T : (i + 1) * T] = high
        ft[T : 2 * T, i * T : (i + 1) * T] = low
        for k in range(NK):
            at = pl.ds(k * T, T)
            lhs = jnp.concatenate([ops[j, 0:T, at], ops[j, T : 2 * T, at]], axis=1)
            picked = fc[table[k, b]]
            wide = dot(lhs, jnp.concatenate([picked, picked], axis=0))
            high, low = split(wide[:, :T] + wide[:, T:])
            moved[i * T : (i + 1) * T, 2 * k * T : (2 * k + 1) * T] = high
            moved[i * T : (i + 1) * T, (2 * k + 1) * T : (2 * k + 2) * T] = low
    for k in range(NK):
        wide = dot(ft[...], moved[:, 2 * k * T : (2 * k + 2) * T])
        renorm[k] = (wide[:T, :T] + (wide[:T, T:] + wide[T:, :T])) * (1.0 / T)


def newop_kernel(info, own_weights, other_scal, own, other, *outs):
    along_t = jnp.where(info[0] == 0, 4, 1)
    along_q = 5 - along_t
    for m, out in enumerate(outs):
        for t in range(4):
            j = 2 * (t * along_t + (info[1] ^ m) * along_q) + info[0]
            acc = None
            for k in range(NK):
                for weight, renorm in ((own_weights[k, j], own), (other_scal[4 + k, j], other)):
                    term = weight * renorm[k]
                    acc = term if acc is None else acc + term
            out[t] = acc


def per_device(start_state, diagonal, left_ops, right_ops, coupling, integrals):
    start, diag, table = start_state[0], diagonal[0], coupling[0]
    op = lax.axis_index("op")
    core, x, y = op % 2, (op // 2) % 4, op // 8
    quarter, other_quarter = jnp.where(core == 0, x, y), jnp.where(core == 0, y, x)
    chain = lax.axis_index("chain")
    info = jnp.stack([core, quarter, other_quarter, op * (ROWS // 32)]).astype(jnp.int32)
    begins = [(quarter ^ m) * PIECE for m in range(4)]
    positions = [other_quarter ^ m for m in range(4)]
    info, begins, positions, odd, upper, lower = lax.optimization_barrier(
        (info, begins, positions, chain % 2 > 0, chain % 4 > 1, chain < 4)
    )
    lc_shape = shape(HT, 2 * T, NK * T, dtype=BF)
    rc_shape = shape(HT, NK, T, 2 * T, dtype=BF)
    raw = (NK, HT, T, T)
    send, vc, state, lc, rc, lraw, rraw = call(
        start_kernel,
        "start",
        2,
        (info, table, start, left_ops[0], right_ops[0]),
        [shape(HALF, T), SPLIT, VECTOR, lc_shape, rc_shape, shape(*raw), shape(*raw)],
        [pltpu.VMEM((ROWS, T), F32), pltpu.VMEM(raw, F32), pltpu.VMEM(raw, F32)]
        + [pltpu.SemaphoreType.DMA, pltpu.SemaphoreType.DMA((2, HT)), pltpu.SemaphoreType.DMA((2, HT))],
        n_hbm=3,
    )
    keep, lkeep, rkeep = call(
        first_keep_kernel,
        "first_keep",
        2,
        (info, table, vc, lraw, rraw),
        [shape(HALF, T), lc_shape, rc_shape],
        flops=1 << 31,
    )
    pieces = sum_terms(begins, send, keep)
    send, vc, sigma, direct, theta, scale = call(
        first_kernel,
        "first",
        2,
        (info, table, *pieces, state, diag, lc, rc),
        [shape(HALF, T), SPLIT, VECTOR, VECTOR, SCALAR, SCALAR],
        [pltpu.VMEM((ROWS, T), F32)],
    )
    for step in range(1, ITERS):
        keep = call(
            keep_kernel, "keep", 2, (info, table, vc, scale, lkeep, rkeep), [shape(HALF, T)], flops=1 << 31
        )[0]
        pieces = sum_terms(begins, send, keep)
        last = step == ITERS - 1
        ops = (lc, rc, lkeep, rkeep, integrals) if last else (lc, rc)
        send, vc, state, sigma, direct, theta, scale = call(
            functools.partial(step_kernel, last),
            "last" if last else "step",
            2,
            (info, table, *pieces, state, sigma, direct, theta, diag, *ops),
            [SCALAR if last else shape(HALF, T), SPLIT, VECTOR, VECTOR, VECTOR, SCALAR, SCALAR],
            [pltpu.VMEM((ROWS, T), F32)] * 3,
        )
    groups = [[2 * p + c for p in range(16)] for c in range(2)]
    other_scal = lax.ppermute(send, "op", CORE_PAIRS)
    scal = send + other_scal
    scal = lax.all_to_all(jnp.broadcast_to(scal[None], (16, 8, T)), "op", 0, 0, axis_index_groups=groups)
    own_rows, renorm = call(
        renorm_kernel,
        "renorm",
        2,
        (info, table, scal, state, direct, theta, lc, lkeep),
        [shape(ROWS // 32, T), shape(NK, T, T)],
        [
            pltpu.VMEM((ROWS, T), F32),
            pltpu.VMEM((NB, T, 2 * T), BF),
            pltpu.VMEM((2 * T, ROWS), BF),
            pltpu.VMEM((ROWS, 2 * NK * T), BF),
        ],
    )
    other = lax.ppermute(renorm, "op", CORE_PAIRS)
    newops = call(
        newop_kernel,
        "newops",
        3,
        (info, integrals, other_scal, renorm, other),
        [shape(4, T, T)] * 4,
    )
    got = [newops[0]] + along(newops, True)

    def position(at):
        mine, *others = [cut(value, at, 1)[0] for value in got]
        return sum4(mine, others)

    mine = [position(at) for at in positions]
    newop = sum4(mine[0], along(mine, False))
    got = lax.ppermute(newop, "chain", [(i, i ^ 1) for i in range(8)])
    before, pair = jnp.where(odd, got, 0.0), newop + got
    got = lax.ppermute(pair, "chain", [(i, i ^ 2) for i in range(8)])
    before, four = before + jnp.where(upper, got, 0.0), pair + got
    got = lax.ppermute(four, "chain", [(0, 6), (1, 7), (2, 4), (3, 5), (6, 0), (7, 1), (4, 2), (5, 3)])
    environment = newop + before + jnp.where(lower, 0.0, got)
    return (own_rows[None], environment[None, None])


def solution(mesh):
    placed = (
        P("chain", None, None),
        P("chain", None, None),
        P("chain", "op", None, None, None),
        P("chain", "op", None, None, None),
        P("chain", "op", None),
        P("op", None),
    )
    return jax.shard_map(
        per_device,
        mesh=mesh,
        in_specs=placed,
        out_specs=(P("chain", "op", None), P("chain", "op", None, None)),
        check_vma=False,
    )
```

```python
import functools

import jax
import jax.numpy as jnp
from jax import lax
from jax.experimental import pallas as pl
from jax.experimental.pallas import tpu as pltpu
from jax.sharding import PartitionSpec as P

ITERS = 4
T = 128
NB = 16
NK = 4
ROWS = NB * T
HALF = ROWS // 2
HT = NB // 2
PIECE = HALF // 4
COUNT = float(ROWS * T)
BF = jnp.bfloat16
F32 = jnp.float32
VMEM = pl.BlockSpec(memory_space=pltpu.VMEM)
HBM = pl.BlockSpec(memory_space=pltpu.HBM)
SMEM = pl.BlockSpec(memory_space=pltpu.SMEM)


def shape(*dims, dtype=F32):
    return jax.ShapeDtypeStruct(dims, dtype)


def place(y, x, c):
    return (y * 4 + x) * 2 + c


def line_pairs(m, first):
    pairs = []
    for y in range(4):
        for x in range(4):
            for c in range(2):
                along_x = (c == 0) == first
                to = place(y, x ^ m, c) if along_x else place(y ^ m, x, c)
                pairs.append((place(y, x, c), to))
    return pairs


CORE_PAIRS = [(i, i ^ 1) for i in range(32)]


def split(value):
    high = value.astype(BF)
    low = (value - high.astype(F32)).astype(BF)
    return high, low


def dot(a, b):
    return jnp.dot(a, b, preferred_element_type=F32)


def total(acc):
    return jnp.sum(jnp.sum(acc, axis=0, keepdims=True), axis=1, keepdims=True)


def fold(value):
    return jnp.sum(value.reshape(-1, 8, T), axis=0)


STEP = 64


def chunks(rows=ROWS):
    return [pl.ds(i, STEP) for i in range(0, rows, STEP)]


def prepare(left, right, j, lc, rc):
    for k in range(NK):
        high, low = split(left[k, j])
        lc[j, 0:T, k * T : (k + 1) * T] = high
        lc[j, T : 2 * T, k * T : (k + 1) * T] = low
        high, low = split(right[k, j].T)
        rc[j, k, :, 0:T] = high
        rc[j, k, :, T : 2 * T] = low


def tile_inner(b, j, table, vc, rc):
    parts = []
    for k in range(NK):
        picked = vc[table[k, b]]
        weights = jnp.concatenate([rc[j, k], rc[j, k]], axis=0)
        wide = dot(picked, weights)
        parts.append(jnp.concatenate(split(wide[:, :T] + wide[:, T:]), axis=1))
    return jnp.concatenate(parts, axis=0)


def tile_outer(j, lc, inner):
    wide = dot(lc[j], inner)
    return wide[:T, :T] + (wide[:T, T:] + wide[T:, :T])


def half_terms(which, table, vc, lc, rc, out, scale=None, between=None):
    inner = tile_inner(which * HT, 0, table, vc, rc)
    for j in range(HT):
        later = tile_inner(which * HT + j + 1, j + 1, table, vc, rc) if j + 1 < HT else None
        value = tile_outer(j, lc, inner)
        inner = later
        out[j * T : (j + 1) * T, :] = value if scale is None else value * scale
        if between is not None:
            between(j, HT)


def store_split(vc, row, value):
    high, low = split(value)
    at = pl.ds(row % T, STEP)
    vc[row // T, at, 0:T] = high
    vc[row // T, at, T : 2 * T] = low


def keep_kernel(info, table, vc, scale, lc, rc, out):
    half_terms(info[0], table, vc, lc, rc, out, scale[0:1, 0:1])


def first_keep_kernel(info, table, vc, left, right, out, lc, rc):
    prepare(left, right, 0, lc, rc)
    inner = tile_inner(info[0] * HT, 0, table, vc, rc)
    for j in range(HT):
        later = None
        if j + 1 < HT:
            prepare(left, right, j + 1, lc, rc)
            later = tile_inner(info[0] * HT + j + 1, j + 1, table, vc, rc)
        out[j * T : (j + 1) * T, :] = tile_outer(j, lc, inner)
        inner = later


def start_kernel(
    info, table, start_hbm, left, right, send, vc, state, lc, rc, lkeep, rkeep, start, lbuf, rbuf, start_sem, sem, keep_sem
):
    own, other = info[0] * HT, (1 - info[0]) * HT
    start_copy = pltpu.make_async_copy(start_hbm, start, start_sem)
    sends = [
        (
            pltpu.make_async_copy(right.at[:, other + j], rbuf.at[:, j], sem.at[0, j]),
            pltpu.make_async_copy(left.at[:, other + j], lbuf.at[:, j], sem.at[1, j]),
        )
        for j in range(HT)
    ]
    keeps = [
        (
            pltpu.make_async_copy(right.at[:, own + j], rkeep.at[:, j], keep_sem.at[0, j]),
            pltpu.make_async_copy(left.at[:, own + j], lkeep.at[:, j], keep_sem.at[1, j]),
        )
        for j in range(HT)
    ]
    queue = sends[:3]
    for j in range(3, HT):
        queue += [keeps[j - 3], sends[j]]
    queue += keeps[HT - 3 :]

    def begin(count):
        for _ in range(count):
            if queue:
                for copy in queue.pop(0):
                    copy.start()

    def ready(j):
        if j < HT:
            for copy in sends[j]:
                copy.wait()
            begin(2)
            prepare(lbuf, rbuf, j, lc, rc)

    begin(1)
    start_copy.start()
    begin(2)
    ready(0)
    ready(1)
    start_copy.wait()
    acc = jnp.zeros((8, T), F32)
    for at in chunks():
        value = start[at, :]
        acc += fold(value * value)
    scale = lax.rsqrt(total(acc) / COUNT + 1e-6)
    for at in chunks():
        value = start[at, :] * scale
        state[at, :] = value
        store_split(vc, at.start, value)
    inner = tile_inner(other, 0, table, vc, rc)
    for j in range(HT):
        ready(j + 2)
        later = tile_inner(other + j + 1, j + 1, table, vc, rc) if j + 1 < HT else None
        send[j * T : (j + 1) * T, :] = tile_outer(j, lc, inner)
        inner = later
    for pair in keeps:
        for copy in pair:
            copy.wait()


def offsets(info):
    own, other = info[0] * HALF, (1 - info[0]) * HALF
    places = [own + (info[1] ^ m) * PIECE for m in (0, 1, 3, 2)]
    places += [other + (info[2] ^ m) * PIECE for m in (0, 1, 3, 2)]
    return places


def next_direct(state, sigma_at, theta, diag, pre, direct, vc):
    acc = jnp.zeros((8, T), F32)
    for at in chunks():
        st, sg = sigma_at(at)
        away = diag[at, :] - theta
        value = (sg - theta * st) * lax.rsqrt(away * away + 1.0)
        pre[at, :] = value
        acc += fold(st * value)
    proj = total(acc) / COUNT
    acc = jnp.zeros((8, T), F32)
    for at in chunks():
        value = pre[at, :] - proj * state[at, :]
        pre[at, :] = value
        store_split(vc, at.start, value)
        acc += fold(value * value)
    scale = lax.rsqrt(total(acc) / COUNT + 1e-6)

    def store(i, count):
        every = chunks()
        for at in every[i * len(every) // count : (i + 1) * len(every) // count]:
            direct[at, :] = pre[at, :] * scale

    return scale, store


def gathered(info, pieces, vector, other, diag, result):
    acc_v, acc_o = jnp.zeros((8, T), F32), jnp.zeros((8, T), F32)
    for piece, begin in zip(pieces, offsets(info), strict=True):
        for here in chunks(PIECE):
            at = pl.ds(pl.multiple_of(begin + here.start, STEP), STEP)
            vec = vector[at, :]
            value = piece[here, :] + diag[at, :] * vec
            result[at, :] = value
            acc_v += fold(vec * value)
            if other is not None:
                acc_o += fold(other[at, :] * value)
    return total(acc_v) / COUNT, total(acc_o) / COUNT


def rotation(theta, bval, cval):
    gap = (theta - bval) / 2.0
    root = jnp.sqrt(gap * gap + cval * cval)
    lam = (theta + bval) / 2.0 - root
    first = bval - lam
    inverse = lax.rsqrt(first * first + cval * cval + 1e-12)
    return lam, first * inverse, cval * inverse


def partial_products(state, direct, diag, table, vc, halves, terms, weights, scal, scale, store):
    tiles = [(which * HT + j, j, lc, rc) for which, lc, rc in halves for j in range(HT)]
    b, j, lc, rc = tiles[0]
    inner = tile_inner(b, j, table, vc, rc)
    for i, (b, j, lc, rc) in enumerate(tiles):
        later = None
        if i + 1 < NB:
            next_b, next_j, _, next_rc = tiles[i + 1]
            later = tile_inner(next_b, next_j, table, vc, next_rc)
        at = pl.ds(pl.multiple_of(b * T, T), T)
        terms[at, :] = tile_outer(j, lc, inner) * scale
        inner = later
        store(i, NB)
    acc_b, acc_c = jnp.zeros((8, T), F32), jnp.zeros((8, T), F32)
    for at in chunks():
        vec = direct[at, :]
        value = terms[at, :] + (1.0 / 32) * (diag[at, :] * vec)
        acc_b += fold(vec * value)
        acc_c += fold(state[at, :] * value)
    scal[...] = jnp.zeros_like(scal)
    scal[0:1, :] = jnp.sum(acc_b, axis=0, keepdims=True)
    scal[1:2, :] = jnp.sum(acc_c, axis=0, keepdims=True)
    scal[4:8, 0:32] = weights[...]


def first_kernel(info, table, *refs):
    pieces, (state, diag, lc, rc, send, vc, sigma, direct, theta_out, scale_out, pre) = refs[:8], refs[8:]
    theta, _ = gathered(info, pieces, state, None, diag, sigma)
    theta_out[...] = jnp.broadcast_to(theta, theta_out.shape)
    scale, store = next_direct(state, lambda at: (state[at, :], sigma[at, :]), theta, diag, pre, direct, vc)
    scale_out[...] = jnp.broadcast_to(scale, scale_out.shape)
    half_terms(1 - info[0], table, vc, lc, rc, send, scale, store)


def step_kernel(last, info, table, *refs):
    pieces, refs = refs[:8], refs[8:]
    state, sigma, direct, theta, diag, lc, rc = refs[:7]
    refs = refs[7:]
    if last:
        (lkeep, rkeep, weights), refs = refs[:3], refs[3:]
    out, vc, state_out, sigma_out, direct_out, theta_out, scale_out, pre, hdirect, terms = refs
    bval, cval = gathered(info, pieces, direct, state, diag, hdirect)
    lam, first, second = rotation(theta[0:1, 0:1], bval, cval)
    theta_out[...] = jnp.broadcast_to(lam, theta_out.shape)

    def updated(at):
        st = first * state[at, :] - second * direct[at, :]
        sg = first * sigma[at, :] - second * hdirect[at, :]
        state_out[at, :] = st
        sigma_out[at, :] = sg
        return st, sg

    scale, store = next_direct(state_out, updated, lam, diag, pre, direct_out, vc)
    scale_out[...] = jnp.broadcast_to(scale, scale_out.shape)
    if last:
        halves = ((1 - info[0], lc, rc), (info[0], lkeep, rkeep))
        partial_products(state_out, direct_out, diag, table, vc, halves, terms, weights, out, scale, store)
    else:
        half_terms(1 - info[0], table, vc, lc, rc, out, scale, store)


VECTOR = shape(ROWS, T)
SPLIT = shape(NB, T, 2 * T, dtype=BF)
SCALAR = shape(8, T)


def call(kernel, name, n_smem, args, outs, scratch=(), flops=0, n_hbm=0, mib=24):
    n_vmem = len(args) - n_smem - n_hbm
    hbm = [pltpu.with_memory_space_constraint(arg, pltpu.HBM) for arg in args[n_smem + n_vmem :]]
    return pl.pallas_call(
        kernel,
        in_specs=[SMEM] * n_smem + [VMEM] * n_vmem + [HBM] * n_hbm,
        out_specs=[VMEM] * len(outs),
        out_shape=[pltpu.VMEM(out.shape, out.dtype) for out in outs],
        scratch_shapes=list(scratch),
        compiler_params=pltpu.CompilerParams(vmem_limit_bytes=mib << 20),
        cost_estimate=pl.CostEstimate(flops=flops, bytes_accessed=1 << 20, transcendentals=0),
        name=name,
    )(*args[: n_smem + n_vmem], *hbm)


def sum4(own, got):
    return (own + got[0]) + (got[2] + got[1])


def along(values, first):
    return [lax.ppermute(values[m], "op", line_pairs(m, first)) for m in (1, 3, 2)]


def cut(value, at, count):
    begin = [at] + [jnp.zeros_like(at)] * (value.ndim - 1)
    return lax.dynamic_slice(value, begin, (count, *value.shape[1:]), allow_negative_indices=False)


def sum_terms(begins, send, keep):
    got = lax.ppermute(send, "op", CORE_PAIRS)

    mine = [cut(keep, at, PIECE) + cut(got, at, PIECE) for at in begins]
    part = sum4(mine[0], along(mine, True))
    whole = sum4(part, along([part] * 4, False))
    far, last, near = [lax.ppermute(whole, "op", line_pairs(m, True)) for m in (2, 3, 1)]
    own = [whole, near, last, far]
    return own + [lax.ppermute(value, "op", CORE_PAIRS) for value in own]


def renorm_kernel(info, table, scal, state, direct, theta, lc, lkeep, rows, renorm, final, fc, ft, moved):
    acc = jnp.sum(scal[...], axis=0)
    bval = jnp.sum(acc[0:1, :], axis=1, keepdims=True) / COUNT
    cval = jnp.sum(acc[1:2, :], axis=1, keepdims=True) / COUNT
    _, first, second = rotation(theta[0:1, 0:1], bval, cval)
    for at in chunks():
        value = first * state[at, :] - second * direct[at, :]
        final[at, :] = value
        store_split(fc, at.start, value)
    rows[...] = final[pl.ds(pl.multiple_of(info[3], ROWS // 32), ROWS // 32), :]
    order = [((1 - info[0]) * HT + j, lc, j) for j in range(HT)] + [(info[0] * HT + j, lkeep, j) for j in range(HT)]
    for i, (b, ops, j) in enumerate(order):
        high, low = split(final[pl.ds(pl.multiple_of(b * T, T), T), :].T)
        ft[0:T, i * T : (i + 1) * T] = high
        ft[T : 2 * T, i * T : (i + 1) * T] = low
        for k in range(NK):
            at = pl.ds(k * T, T)
            lhs = jnp.concatenate([ops[j, 0:T, at], ops[j, T : 2 * T, at]], axis=1)
            picked = fc[table[k, b]]
            wide = dot(lhs, jnp.concatenate([picked, picked], axis=0))
            high, low = split(wide[:, :T] + wide[:, T:])
            moved[i * T : (i + 1) * T, 2 * k * T : (2 * k + 1) * T] = high
            moved[i * T : (i + 1) * T, (2 * k + 1) * T : (2 * k + 2) * T] = low
    for k in range(NK):
        wide = dot(ft[...], moved[:, 2 * k * T : (2 * k + 2) * T])
        renorm[k] = (wide[:T, :T] + (wide[:T, T:] + wide[T:, :T])) * (1.0 / T)


def newop_kernel(info, own_weights, other_scal, own, other, *outs):
    along_t = jnp.where(info[0] == 0, 4, 1)
    along_q = 5 - along_t
    for m, out in enumerate(outs):
        for t in range(4):
            j = 2 * (t * along_t + (info[1] ^ m) * along_q) + info[0]
            acc = None
            for k in range(NK):
                for weight, renorm in ((own_weights[k, j], own), (other_scal[4 + k, j], other)):
                    term = weight * renorm[k]
                    acc = term if acc is None else acc + term
            out[t] = acc


def per_device(start_state, diagonal, left_ops, right_ops, coupling, integrals):
    start, diag, table = start_state[0], diagonal[0], coupling[0]
    op = lax.axis_index("op")
    core, x, y = op % 2, (op // 2) % 4, op // 8
    quarter, other_quarter = jnp.where(core == 0, x, y), jnp.where(core == 0, y, x)
    chain = lax.axis_index("chain")
    info = jnp.stack([core, quarter, other_quarter, op * (ROWS // 32)]).astype(jnp.int32)
    begins = [(quarter ^ m) * PIECE for m in range(4)]
    positions = [other_quarter ^ m for m in range(4)]
    info, begins, positions, odd, upper, lower = lax.optimization_barrier(
        (info, begins, positions, chain % 2 > 0, chain % 4 > 1, chain < 4)
    )
    lc_shape = shape(HT, 2 * T, NK * T, dtype=BF)
    rc_shape = shape(HT, NK, T, 2 * T, dtype=BF)
    raw = (NK, HT, T, T)
    send, vc, state, lc, rc, lraw, rraw = call(
        start_kernel,
        "start",
        2,
        (info, pltpu.with_memory_space_constraint(table, pltpu.HBM), start, left_ops[0], right_ops[0]),
        [shape(HALF, T), SPLIT, VECTOR, lc_shape, rc_shape, shape(*raw), shape(*raw)],
        [pltpu.VMEM((ROWS, T), F32), pltpu.VMEM(raw, F32), pltpu.VMEM(raw, F32)]
        + [pltpu.SemaphoreType.DMA, pltpu.SemaphoreType.DMA((2, HT)), pltpu.SemaphoreType.DMA((2, HT))],
        n_hbm=3,
    )
    keep, lkeep, rkeep = call(
        first_keep_kernel,
        "first_keep",
        2,
        (info, table, vc, lraw, rraw),
        [shape(HALF, T), lc_shape, rc_shape],
        flops=1 << 31,
    )
    pieces = sum_terms(begins, send, keep)
    send, vc, sigma, direct, theta, scale = call(
        first_kernel,
        "first",
        2,
        (info, table, *pieces, state, diag, lc, rc),
        [shape(HALF, T), SPLIT, VECTOR, VECTOR, SCALAR, SCALAR],
        [pltpu.VMEM((ROWS, T), F32)],
    )
    for step in range(1, ITERS):
        keep = call(
            keep_kernel, "keep", 2, (info, table, vc, scale, lkeep, rkeep), [shape(HALF, T)], flops=1 << 31
        )[0]
        pieces = sum_terms(begins, send, keep)
        last = step == ITERS - 1
        ops = (lc, rc, lkeep, rkeep, integrals) if last else (lc, rc)
        send, vc, state, sigma, direct, theta, scale = call(
            functools.partial(step_kernel, last),
            "last" if last else "step",
            2,
            (info, table, *pieces, state, sigma, direct, theta, diag, *ops),
            [SCALAR if last else shape(HALF, T), SPLIT, VECTOR, VECTOR, VECTOR, SCALAR, SCALAR],
            [pltpu.VMEM((ROWS, T), F32)] * 3,
        )
    groups = [[2 * p + c for p in range(16)] for c in range(2)]
    other_scal = lax.ppermute(send, "op", CORE_PAIRS)
    scal = send + other_scal
    scal = lax.all_to_all(jnp.broadcast_to(scal[None], (16, 8, T)), "op", 0, 0, axis_index_groups=groups)
    own_rows, renorm = call(
        renorm_kernel,
        "renorm",
        2,
        (info, table, scal, state, direct, theta, lc, lkeep),
        [shape(ROWS // 32, T), shape(NK, T, T)],
        [
            pltpu.VMEM((ROWS, T), F32),
            pltpu.VMEM((NB, T, 2 * T), BF),
            pltpu.VMEM((2 * T, ROWS), BF),
            pltpu.VMEM((ROWS, 2 * NK * T), BF),
        ],
    )
    other = lax.ppermute(renorm, "op", CORE_PAIRS)
    newops = call(
        newop_kernel,
        "newops",
        3,
        (info, integrals, other_scal, renorm, other),
        [shape(4, T, T)] * 4,
    )
    got = [newops[0]] + along(newops, True)

    def position(at):
        mine, *others = [cut(value, at, 1)[0] for value in got]
        return sum4(mine, others)

    mine = [position(at) for at in positions]
    newop = sum4(mine[0], along(mine, False))
    got = lax.ppermute(newop, "chain", [(i, i ^ 1) for i in range(8)])
    before, pair = jnp.where(odd, got, 0.0), newop + got
    got = lax.ppermute(pair, "chain", [(i, i ^ 2) for i in range(8)])
    before, four = before + jnp.where(upper, got, 0.0), pair + got
    got = lax.ppermute(four, "chain", [(0, 6), (1, 7), (2, 4), (3, 5), (6, 0), (7, 1), (4, 2), (5, 3)])
    environment = newop + before + jnp.where(lower, 0.0, got)
    return (own_rows[None], environment[None, None])


def solution(mesh):
    placed = (
        P("chain", None, None),
        P("chain", None, None),
        P("chain", "op", None, None, None),
        P("chain", "op", None, None, None),
        P("chain", "op", None),
        P("op", None),
    )
    return jax.shard_map(
        per_device,
        mesh=mesh,
        in_specs=placed,
        out_specs=(P("chain", "op", None), P("chain", "op", None, None)),
        check_vma=False,
    )
```
